32 devices in a mesh: ctx: 4 (over z), tp: 4 (over x, core), dp: 2 (over y).
Axes of the slice: x: 2, y: 2, z: 4, core: 2. Of those that a mesh axis runs over, the one named last changes fastest.
Arguments:
- queries: bfloat16 [512, 8192], P(('dp', 'ctx'), 'tp'), parts along dimension 0, may hold values from -12 to 12
- cache_keys: bfloat16 [4096, 1024], P(('dp', 'ctx'), 'tp'), parts along dimension 0, may hold values from -4 to 4
- cache_values: bfloat16 [4096, 1024], P(('dp', 'ctx'), 'tp'), parts along dimension 0, may hold values from -6 to 6
- new_keys: bfloat16 [512, 1024], P(('dp', 'ctx'), 'tp'), parts along dimension 0, may hold values from -6 to 6
- new_values: bfloat16 [512, 1024], P(('dp', 'ctx'), 'tp'), parts along dimension 0, may hold values from -6 to 6
- prefix_len: int32 [2], P('dp'), parts along dimension 0, may hold values from 1024 to 2048
Outputs:
- attended: bfloat16 [512, 8192], P(('dp', 'ctx'), 'tp'), parts along dimension 0
The draws below stay inside these ranges and needn't reach their ends.
There are 2 independent parts, one for each index of `dp`. The reference program is written for one: setup_inputs(seed, part) draws one part's arguments, and reference() takes and returns one part's arrays. A program takes and returns all parts, laid end to end along the dimension named above; each array names one. Nothing has to cross between parts.
All inputs are finite; a program needn't handle non-finite values.
Results may differ from the reference program's by a relative error of at most 0.038.
Values may be sent and summed in bfloat16 or wider, within the bound.
No kernel may reach another device: no remote copies, remote signals or barrier semaphores. Data moves between devices by JAX's collectives and lax.ppermute only.
A program may use at most 64 MiB of HBM per device.

```python
import jax
import jax.numpy as jnp
from jax import lax

HEADS = 64
KV_HEADS = 8
HEAD_DIM = 128
GROUP = 8
SPAN = 256
CACHE = 2048


def draw_queries(key, part):
    drawn = 2.0 * jnp.clip(jax.random.normal(jax.random.fold_in(key, 12), (SPAN, HEADS * HEAD_DIM), jnp.float32), -6.0, 6.0)
    return drawn.astype(jnp.bfloat16)


def draw_cache_keys(key, part):
    drawn = jnp.clip(jax.random.normal(jax.random.fold_in(key, 22), (CACHE, KV_HEADS * HEAD_DIM), jnp.float32), -4.0, 4.0)
    return drawn.astype(jnp.bfloat16)


def block_scale(stream_key, shape, pieces, least, high):
    gain, own = 1.0, jax.random.fold_in(stream_key, 6)
    for axis_at, shards_of in pieces:
        draws = jnp.exp(jax.random.uniform(jax.random.fold_in(own, axis_at), (shards_of,), jnp.float32, least / len(pieces), high / len(pieces)))
        gain = gain * jnp.repeat(draws, shape[axis_at] // shards_of).reshape([-1 if axis == axis_at else 1 for axis in range(len(shape))])
    return gain


def noise(rng, extent, deviation, reach, cuts=(), held_as=jnp.bfloat16):
    values = jax.random.normal(rng, extent, jnp.float32) * deviation
    if len(cuts) > 0:
        values = block_scale(rng, extent, cuts, -0.22, 0.18) * values
    return jnp.clip(values, min=-reach, max=reach).astype(held_as)


def setup_inputs(seed: int = 0, part: int = 0) -> dict:
    streams_of = jax.random.split(jax.random.key(seed), 7)
    part_splits = jax.random.split(jax.random.fold_in(streams_of[6], part), 7)
    queries = draw_queries(jax.random.fold_in(jax.random.fold_in(streams_of[6], part), 71), part)
    cache_keys = draw_cache_keys(jax.random.fold_in(jax.random.fold_in(streams_of[6], part), 71), part)
    cache_values = noise(part_splits[2], (CACHE, KV_HEADS * HEAD_DIM), 1.0, 6.0, ((0, 4), (1, 4)))
    new_keys = noise(part_splits[3], (SPAN, KV_HEADS * HEAD_DIM), 1.0, 6.0, ((0, 4), (1, 4)))
    new_values = noise(part_splits[4], (SPAN, KV_HEADS * HEAD_DIM), 1.0, 6.0, ((0, 4), (1, 4)))
    prefix_len = jax.random.randint(part_splits[5], (1,), CACHE // 2, CACHE + 1).astype(jnp.int32)
    return {"queries": queries, "cache_keys": cache_keys, "cache_values": cache_values, "new_keys": new_keys, "new_values": new_values, "prefix_len": prefix_len}


def reference(queries, cache_keys, cache_values, new_keys, new_values, prefix_len):
    length = prefix_len[0]
    all_rows = CACHE + SPAN
    all_keys = jnp.concatenate([cache_keys, new_keys], 0)
    all_values = jnp.concatenate([cache_values, new_values], 0)
    key_index = jnp.arange(all_rows, dtype=jnp.int32)
    query_pos = jnp.arange(SPAN, dtype=jnp.int32)
    allowed = jnp.where(key_index[None, :] < CACHE, key_index[None, :] < length,
                        (key_index[None, :] - CACHE) <= query_pos[:, None])
    grouped = queries.reshape(SPAN, KV_HEADS, GROUP, HEAD_DIM).transpose(1, 0, 2, 3)
    key_heads = all_keys.reshape(all_rows, KV_HEADS, HEAD_DIM).transpose(1, 0, 2)
    value_heads = all_values.reshape(all_rows, KV_HEADS, HEAD_DIM).transpose(1, 0, 2)
    scale = HEAD_DIM ** -0.5

    def one_head(head_inputs):
        query_part, key_part, value_part = head_inputs
        scores = jnp.einsum('cpd,kd->cpk', query_part.astype(jnp.float32), key_part.astype(jnp.float32)) * scale
        scores = jnp.where(allowed[:, None, :], scores, jnp.float32(-1e30))
        largest = jnp.max(scores, -1, keepdims=True)
        weights = jnp.where(allowed[:, None, :], jnp.exp(scores - largest), jnp.float32(0.0))
        denominator = jnp.sum(weights, -1)
        rounded = lax.optimization_barrier(weights.astype(jnp.bfloat16))
        numerator = jnp.einsum('cpk,kd->cpd', rounded.astype(jnp.float32), value_part.astype(jnp.float32))
        return numerator / denominator[..., None]

    result = lax.map(one_head, (grouped, key_heads, value_heads))
    return result.transpose(1, 0, 2, 3).reshape(SPAN, HEADS * HEAD_DIM).astype(jnp.bfloat16)
```

```python
import functools

import jax
import jax.numpy as jnp
from jax import lax
from jax.experimental import pallas as pl
from jax.experimental.pallas import tpu as pltpu
from jax.sharding import PartitionSpec as P

HEAD_DIM = 128
LOW = -1e30
SLOPE = HEAD_DIM ** (-0.5) * 1.4426950408889634
STATS = 16
TRADES = ((1, 2), (2, 1))

VMEM = pl.BlockSpec(memory_space=pltpu.VMEM)
SMEM = pl.BlockSpec(memory_space=pltpu.SMEM)
ANY = pl.BlockSpec(memory_space=pl.ANY)
LIMIT = 24 * 1024 * 1024


def lead(array, row):
    return array[row : row + 1, :]


def attend(query, kv_ref, source, token_dev, length, cache_rows, new_rows, lane0):
    key_rows = cache_rows + new_rows
    keys = kv_ref[0:key_rows, :]
    scores = lax.dot_general(
        keys, query, (((1,), (1,)), ((), ())), preferred_element_type=jnp.float32
    )
    rows = query.shape[0]
    slot = lax.broadcasted_iota(jnp.int32, (cache_rows, rows), 0)
    cached = jnp.where(slot < length - source * cache_rows, scores[:cache_rows], LOW)
    new = lax.broadcasted_iota(jnp.int32, (new_rows, rows), 0) + source * new_rows
    token = lax.rem(
        lax.broadcasted_iota(jnp.int32, (new_rows, rows), 1), new_rows
    ) + token_dev * new_rows
    fresh = jnp.where(new <= token, scores[cache_rows:], LOW)
    scores = jnp.concatenate([cached, fresh], 0)
    top = jnp.max(scores, axis=0, keepdims=True)
    weights = jnp.exp2((scores - top) * SLOPE)
    total = jnp.sum(weights, axis=0, keepdims=True)
    values = kv_ref[key_rows : 2 * key_rows, :]
    summed = lax.dot_general(
        values,
        weights.astype(jnp.bfloat16),
        (((0,), (0,)), ((), ())),
        preferred_element_type=jnp.float32,
    )
    return top, total, summed


def joined(one, two):
    top = jnp.maximum(one[0], two[0])
    left, right = jnp.exp2((one[0] - top) * SLOPE), jnp.exp2((two[0] - top) * SLOPE)
    return top, one[1] * left + two[1] * right, one[2] * left + two[2] * right


def stacked_heads(q_ref, first, count):
    return jnp.concatenate(
        [q_ref[:, pl.ds((first + g) * HEAD_DIM, HEAD_DIM)] for g in range(count)], 0
    )


def start_kernel(dims, kv_xor, q_xor, len_ref, q_ref, kv_ref, state_ref):
    cache_rows, new_rows, groups, step = dims
    me = lax.axis_index("ctx")
    for at in range(0, groups, step):
        query = stacked_heads(q_ref, at, step)
        lanes = pl.ds(at * new_rows, step * new_rows)
        top, total, summed = attend(
            query, kv_ref, me ^ kv_xor, me ^ q_xor, len_ref[0], cache_rows, new_rows, at
        )
        state_ref[0:HEAD_DIM, lanes] = summed
        state_ref[HEAD_DIM : HEAD_DIM + 1, lanes] = top
        state_ref[HEAD_DIM + 1 : HEAD_DIM + 2, lanes] = total


def finish_kernel(dims, kv_xor, q_xor, packed, len_ref, q_ref, kv_ref, state_ref, out_ref):
    cache_rows, new_rows, groups, step = dims
    me = lax.axis_index("ctx")
    for at in range(0, groups, step):
        query = stacked_heads(q_ref, at, step)
        lanes = pl.ds(at * new_rows, step * new_rows)
        ours = attend(
            query, kv_ref, me ^ kv_xor, me ^ q_xor, len_ref[0], cache_rows, new_rows, at
        )
        before = (
            state_ref[HEAD_DIM : HEAD_DIM + 1, lanes],
            state_ref[HEAD_DIM + 1 : HEAD_DIM + 2, lanes],
            state_ref[0:HEAD_DIM, lanes],
        )
        top, total, summed = joined(before, ours)
        result = summed * (1.0 / total)
        log = top * SLOPE + jnp.log2(total)
        if packed:
            high = log.astype(jnp.bfloat16).astype(jnp.float32)
            rest = log - high
            middle = rest.astype(jnp.bfloat16).astype(jnp.float32)
            low = rest - middle
            row = lax.broadcasted_iota(jnp.int32, (STATS, step * new_rows), 0)
            stats = jnp.where(row == 0, high, jnp.where(row == 1, middle, jnp.where(row == 2, low, 0.0)))
            out_ref[0:HEAD_DIM, lanes] = result.astype(jnp.bfloat16)
            out_ref[HEAD_DIM : HEAD_DIM + STATS, lanes] = stats.astype(jnp.bfloat16)
        else:
            out_ref[0:HEAD_DIM, lanes] = result
            out_ref[HEAD_DIM : HEAD_DIM + 1, lanes] = log


def merge_kernel(dims, heads, *refs):
    cache_rows, new_rows, groups, step = dims
    out_ref = refs[-1]
    pair = HEAD_DIM // new_rows
    for head in range(heads):
        own_ref, got_ref = refs[2 * head], refs[2 * head + 1]
        for at in range(0, groups, pair):
            lanes = pl.ds(at * new_rows, pair * new_rows)
            stats = got_ref[HEAD_DIM : HEAD_DIM + STATS, lanes].astype(jnp.float32)
            theirs = stats[0:1] + stats[1:2] + stats[2:3]
            mine = own_ref[HEAD_DIM : HEAD_DIM + 1, lanes]
            top = jnp.maximum(mine, theirs)
            left, right = jnp.exp2(mine - top), jnp.exp2(theirs - top)
            scale = 1.0 / (left + right)
            whole = own_ref[0:HEAD_DIM, lanes] * (left * scale) + got_ref[
                0:HEAD_DIM, lanes
            ].astype(jnp.float32) * (right * scale)
            turned = whole.T.astype(jnp.bfloat16)
            for g in range(pair):
                column = (head * groups + at + g) * HEAD_DIM
                out_ref[:, column : column + HEAD_DIM] = turned[g * new_rows : (g + 1) * new_rows, :]


def pack_kernel(heads, q_ref, ck_ref, cv_ref, nk_ref, nv_ref, *rest):
    sems = rest[-1]
    kv_refs, q_refs = rest[0:heads], rest[heads : 2 * heads]
    cache_rows, new_rows = ck_ref.shape[0], nk_ref.shape[0]
    key_rows = cache_rows + new_rows
    width = q_ref.shape[1] // heads
    copies = []
    for head in range(heads):
        columns = pl.ds(head * HEAD_DIM, HEAD_DIM)
        kv = kv_refs[head]
        for source, at, rows in (
            (ck_ref, 0, cache_rows),
            (nk_ref, cache_rows, new_rows),
            (cv_ref, key_rows, cache_rows),
            (nv_ref, key_rows + cache_rows, new_rows),
        ):
            copies.append((source.at[:, columns], kv.at[pl.ds(at, rows), :]))
        copies.append((q_ref.at[:, pl.ds(head * width, width)], q_refs[head]))
    handles = [
        pltpu.make_async_copy(source, target, sems.at[n])
        for n, (source, target) in enumerate(copies)
    ]
    for handle in handles:
        handle.start()
    for handle in handles:
        handle.wait()


def traded(value, xor):
    count = lax.axis_size("ctx")
    return lax.ppermute(value, "ctx", [(source, source ^ xor) for source in range(count)])


def cost(dims):
    cache_rows, new_rows, groups, _ = dims
    pairs = (cache_rows + new_rows) * groups * new_rows
    return pl.CostEstimate(
        flops=4 * HEAD_DIM * pairs, bytes_accessed=1 << 20, transcendentals=pairs
    )


def local_four(queries, cache_keys, cache_values, new_keys, new_values, prefix_len):
    cache_rows, kv_width = cache_keys.shape
    new_rows = queries.shape[0]
    heads = kv_width // HEAD_DIM
    groups = queries.shape[1] // kv_width
    key_rows = cache_rows + new_rows
    rows = groups * new_rows
    dims = (cache_rows, new_rows, groups, 4)
    params = pltpu.CompilerParams(vmem_limit_bytes=LIMIT)
    bf16, f32 = jnp.bfloat16, jnp.float32
    packed = pl.pallas_call(
        functools.partial(pack_kernel, heads),
        out_shape=[jax.ShapeDtypeStruct((2 * key_rows, HEAD_DIM), bf16)] * heads
        + [jax.ShapeDtypeStruct((new_rows, groups * HEAD_DIM), bf16)] * heads,
        in_specs=[ANY] * 5,
        out_specs=[ANY] * (2 * heads),
        scratch_shapes=[pltpu.SemaphoreType.DMA((5 * heads,))],
        compiler_params=params,
        name="pack",
    )(queries, cache_keys, cache_values, new_keys, new_values)
    kv, q = packed[:heads], packed[heads:]
    state = jax.ShapeDtypeStruct((HEAD_DIM + 8, rows), f32)
    sent = jax.ShapeDtypeStruct((HEAD_DIM + STATS, rows), bf16)

    def start(head, kv_xor, q_xor, query, keys):
        return pl.pallas_call(
            functools.partial(start_kernel, dims, kv_xor, q_xor),
            out_shape=state,
            in_specs=[SMEM, VMEM, VMEM],
            out_specs=VMEM,
            compiler_params=params,
            cost_estimate=cost(dims),
            name="start",
        )(prefix_len, query, keys)

    def finish(head, kv_xor, q_xor, query, keys, before, out):
        return pl.pallas_call(
            functools.partial(finish_kernel, dims, kv_xor, q_xor, out is sent),
            out_shape=out,
            in_specs=[SMEM, VMEM, VMEM, VMEM],
            out_specs=VMEM,
            compiler_params=params,
            cost_estimate=cost(dims),
            name="finish",
        )(prefix_len, query, keys, before)

    far_q = [traded(q[h], TRADES[h % 2][1]) for h in range(heads)]
    far_kv = [traded(kv[h], TRADES[h % 2][0]) for h in range(heads)]
    mine = [start(h, 0, 0, q[h], kv[h]) for h in range(heads)]
    theirs = [start(h, 0, TRADES[h % 2][1], far_q[h], kv[h]) for h in range(heads)]
    pieces = []
    for h in range(heads):
        kv_xor, q_xor = TRADES[h % 2]
        out = finish(h, kv_xor, q_xor, far_q[h], far_kv[h], theirs[h], sent)
        got = traded(out, q_xor)
        own = finish(h, kv_xor, 0, q[h], far_kv[h], mine[h], state)
        pieces += [own, got]
    return pl.pallas_call(
        functools.partial(merge_kernel, dims, heads),
        out_shape=jax.ShapeDtypeStruct(queries.shape, bf16),
        in_specs=[VMEM] * (2 * heads),
        out_specs=VMEM,
        compiler_params=params,
        name="merge",
    )(*pieces)


def passed_along(value, axis, steps):
    count = lax.axis_size(axis)
    pairs = [(source, (source + steps) % count) for source in range(count)]
    return lax.ppermute(value, axis, pairs)


def allowed_for(source, query_tok, cache_rows, query_rows, length):
    key_rows = cache_rows + query_rows
    key_index = jnp.arange(key_rows, dtype=jnp.int32)
    cache_pos = source * cache_rows + key_index
    new_pos = source * query_rows + key_index - cache_rows
    return jnp.where(
        (key_index < cache_rows)[None, :],
        (cache_pos < length)[None, :],
        new_pos[None, :] <= query_tok[:, None],
    )


def softmax_block(running, query_heads, kv_block, allowed):
    old_max, old_total, old_acc = running
    scale = HEAD_DIM ** (-0.5)
    scores = (
        jnp.einsum("hrd,hkd->hrk", query_heads, kv_block[0], preferred_element_type=jnp.float32)
        * scale
    )
    scores = jnp.where(allowed[None], scores, jnp.float32(-1e30))
    new_max = jnp.maximum(old_max, jnp.max(scores, -1))
    weights = jnp.where(allowed[None], jnp.exp(scores - new_max[..., None]), jnp.float32(0.0))
    rescale = jnp.exp(old_max - new_max)
    new_total = old_total * rescale + jnp.sum(weights, -1)
    new_acc = old_acc * rescale[..., None] + jnp.einsum(
        "hrk,hkd->hrd",
        weights.astype(jnp.bfloat16),
        kv_block[1],
        preferred_element_type=jnp.float32,
    )
    return (new_max, new_total, new_acc)


def empty_state(heads, rows):
    return (
        jnp.full((heads, rows), -1e30, jnp.float32),
        jnp.zeros((heads, rows), jnp.float32),
        jnp.zeros((heads, rows, HEAD_DIM), jnp.float32),
    )


def local_ring(queries, cache_keys, cache_values, new_keys, new_values, prefix_len):
    length = prefix_len[0]
    cycle_size = lax.axis_size("ctx")
    my_index = lax.axis_index("ctx")
    cache_rows = cache_keys.shape[0]
    query_rows = queries.shape[0]
    kv_width = cache_keys.shape[1]
    kv_heads = kv_width // HEAD_DIM
    groups = queries.shape[1] // kv_width
    key_rows = cache_rows + query_rows
    stacked = jnp.stack(
        [jnp.concatenate([cache_keys, new_keys], 0), jnp.concatenate([cache_values, new_values], 0)]
    )
    kv_block = stacked.reshape(2, key_rows, kv_heads, HEAD_DIM).transpose(0, 2, 1, 3)
    query_heads = (
        queries.reshape(query_rows, kv_heads, groups, HEAD_DIM)
        .transpose(1, 0, 2, 3)
        .reshape(kv_heads, query_rows * groups, HEAD_DIM)
    )
    query_tok = my_index * query_rows + jnp.arange(query_rows * groups, dtype=jnp.int32) // groups
    running = softmax_block(
        empty_state(kv_heads, query_rows * groups),
        query_heads,
        kv_block,
        allowed_for(my_index, query_tok, cache_rows, query_rows, length),
    )

    def one_turn(turn_index, loop_state):
        running_now, held = loop_state
        held = passed_along(held, "ctx", 1)
        source = (my_index - turn_index) % cycle_size
        allowed = allowed_for(source, query_tok, cache_rows, query_rows, length)
        return (softmax_block(running_now, query_heads, held, allowed), held)

    running, held = lax.fori_loop(1, cycle_size, one_turn, (running, kv_block))
    final_max, final_total, final_acc = running
    result = final_acc / final_total[..., None]
    result = result.reshape(kv_heads, query_rows, groups, HEAD_DIM).transpose(1, 0, 2, 3)
    return result.reshape(query_rows, kv_width * groups).astype(jnp.bfloat16)


def solution(mesh):
    in_specs = (
        P(("dp", "ctx"), "tp"),
        P(("dp", "ctx"), "tp"),
        P(("dp", "ctx"), "tp"),
        P(("dp", "ctx"), "tp"),
        P(("dp", "ctx"), "tp"),
        P("dp"),
    )
    out_specs = P(("dp", "ctx"), "tp")
    local = local_four if mesh.shape["ctx"] == 4 else local_ring
    return jax.shard_map(local, mesh=mesh, in_specs=in_specs, out_specs=out_specs, check_vma=False)
```

```python
import functools

import jax
import jax.numpy as jnp
from jax import lax
from jax.experimental import pallas as pl
from jax.experimental.pallas import tpu as pltpu
from jax.sharding import PartitionSpec as P

HEAD_DIM = 128
LOW = -1e30
SLOPE = HEAD_DIM ** (-0.5) * 1.4426950408889634
STATS = 16
STEP = 4

VMEM = pl.BlockSpec(memory_space=pltpu.VMEM)
SMEM = pl.BlockSpec(memory_space=pltpu.SMEM)
HBM = pl.BlockSpec(memory_space=pltpu.HBM)
ANY = pl.BlockSpec(memory_space=pl.ANY)
LIMIT = 24 * 1024 * 1024


def attend(query, kv_ref, source, token_dev, length, cache_rows, new_rows):
    key_rows = cache_rows + new_rows
    keys = kv_ref[0:key_rows, :]
    scores = lax.dot_general(
        keys, query, (((1,), (1,)), ((), ())), preferred_element_type=jnp.float32
    )
    rows = query.shape[0]
    slot = lax.broadcasted_iota(jnp.int32, (cache_rows, rows), 0)
    cached = jnp.where(slot < length - source * cache_rows, scores[:cache_rows], LOW)
    new = lax.broadcasted_iota(jnp.int32, (new_rows, rows), 0) + source * new_rows
    token = lax.rem(
        lax.broadcasted_iota(jnp.int32, (new_rows, rows), 1), new_rows
    ) + token_dev * new_rows
    fresh = jnp.where(new <= token, scores[cache_rows:], LOW)
    scores = jnp.concatenate([cached, fresh], 0)
    top = jnp.max(scores, axis=0, keepdims=True)
    weights = jnp.exp2((scores - top) * SLOPE)
    total = jnp.sum(weights, axis=0, keepdims=True)
    values = kv_ref[key_rows : 2 * key_rows, :]
    summed = lax.dot_general(
        values,
        weights.astype(jnp.bfloat16),
        (((0,), (0,)), ((), ())),
        preferred_element_type=jnp.float32,
    )
    return top, total, summed


def joined(one, two):
    top = jnp.maximum(one[0], two[0])
    left, right = jnp.exp2((one[0] - top) * SLOPE), jnp.exp2((two[0] - top) * SLOPE)
    return top, one[1] * left + two[1] * right, one[2] * left + two[2] * right


def stacked_heads(q_ref, first, count):
    return jnp.concatenate(
        [q_ref[:, pl.ds((first + g) * HEAD_DIM, HEAD_DIM)] for g in range(count)], 0
    )


def load_state(ref, lanes):
    return (
        ref[HEAD_DIM : HEAD_DIM + 1, lanes],
        ref[HEAD_DIM + 1 : HEAD_DIM + 2, lanes],
        ref[0:HEAD_DIM, lanes],
    )


def store_state(ref, lanes, state):
    top, total, summed = state
    ref[0:HEAD_DIM, lanes] = summed
    ref[HEAD_DIM : HEAD_DIM + 1, lanes] = top
    ref[HEAD_DIM + 1 : HEAD_DIM + 2, lanes] = total


def store_own(ref, lanes, state):
    top, total, summed = state
    ref[0:HEAD_DIM, lanes] = summed * (1.0 / total)
    ref[HEAD_DIM : HEAD_DIM + 1, lanes] = top * SLOPE + jnp.log2(total)


def store_sent(ref, lanes, state):
    top, total, summed = state
    log = top * SLOPE + jnp.log2(total)
    high = log.astype(jnp.bfloat16).astype(jnp.float32)
    rest = log - high
    middle = rest.astype(jnp.bfloat16).astype(jnp.float32)
    row = lax.broadcasted_iota(jnp.int32, (STATS, log.shape[1]), 0)
    stats = jnp.where(
        row == 0, high, jnp.where(row == 1, middle, jnp.where(row == 2, rest - middle, 0.0))
    )
    ref[0:HEAD_DIM, lanes] = (summed * (1.0 / total)).astype(jnp.bfloat16)
    ref[HEAD_DIM : HEAD_DIM + STATS, lanes] = stats.astype(jnp.bfloat16)


STORES = {"state": store_state, "own": store_own, "sent": store_sent}


def attend_kernel(dims, blocks, q_xor, store, carried, after, len_ref, q_ref, *refs):
    cache_rows, new_rows, step = dims
    kv_refs, out_ref = refs[: len(blocks)], refs[-1]
    me = lax.axis_index("ctx")
    groups = q_ref.shape[1] // HEAD_DIM
    for at in range(0, groups, step):
        query = stacked_heads(q_ref, at, step)
        lanes = pl.ds(at * new_rows, step * new_rows)
        state = load_state(refs[len(blocks)], lanes) if carried else None
        for block, kv_ref in zip(blocks, kv_refs):
            ours = attend(
                query, kv_ref, me ^ block, me ^ q_xor, len_ref[0], cache_rows, new_rows
            )
            state = ours if state is None else joined(state, ours)
        STORES[store](out_ref, lanes, state)


def merge_kernel(dims, columns, aliased, own_ref, got_ref, *refs):
    cache_rows, new_rows, _ = dims
    out_ref, block_ref, sem = refs[-3:]
    first, own_first, groups = columns
    pair = HEAD_DIM // new_rows
    for at in range(0, groups, pair):
        lanes = pl.ds(at * new_rows, pair * new_rows)
        own_lanes = pl.ds((own_first + at) * new_rows, pair * new_rows)
        stats = got_ref[HEAD_DIM : HEAD_DIM + STATS, lanes].astype(jnp.float32)
        theirs = stats[0:1] + stats[1:2] + stats[2:3]
        mine = own_ref[HEAD_DIM : HEAD_DIM + 1, own_lanes]
        top = jnp.maximum(mine, theirs)
        left, right = jnp.exp2(mine - top), jnp.exp2(theirs - top)
        scale = 1.0 / (left + right)
        whole = own_ref[0:HEAD_DIM, own_lanes] * (left * scale) + got_ref[
            0:HEAD_DIM, lanes
        ].astype(jnp.float32) * (right * scale)
        turned = whole.T.astype(jnp.bfloat16)
        for g in range(pair):
            column = (at + g) * HEAD_DIM
            block_ref[:, column : column + HEAD_DIM] = turned[g * new_rows : (g + 1) * new_rows, :]
    copy = pltpu.make_async_copy(
        block_ref, out_ref.at[:, pl.ds(first * HEAD_DIM, groups * HEAD_DIM)], sem
    )
    copy.start()
    copy.wait()


def pack_kernel(head, pieces, q_ref, ck_ref, cv_ref, nk_ref, nv_ref, *rest):
    sems = rest[-1]
    kv, q_refs = rest[-2 - pieces], rest[-1 - pieces : -1]
    cache_rows, new_rows = ck_ref.shape[0], nk_ref.shape[0]
    key_rows = cache_rows + new_rows
    width = q_refs[0].shape[1]
    columns = pl.ds(head * HEAD_DIM, HEAD_DIM)
    copies = [
        (source.at[:, columns], kv.at[pl.ds(at, rows), :])
        for source, at, rows in (
            (ck_ref, 0, cache_rows),
            (nk_ref, cache_rows, new_rows),
            (cv_ref, key_rows, cache_rows),
            (nv_ref, key_rows + cache_rows, new_rows),
        )
    ] + [
        (q_ref.at[:, pl.ds((head * pieces + piece) * width, width)], q_refs[piece])
        for piece in range(pieces)
    ]
    handles = [
        pltpu.make_async_copy(source, target, sems.at[n])
        for n, (source, target) in enumerate(copies)
    ]
    for handle in handles:
        handle.start()
    for handle in handles:
        handle.wait()


def traded(value, xor):
    count = lax.axis_size("ctx")
    return lax.ppermute(value, "ctx", [(source, source ^ xor) for source in range(count)])


def local_four(queries, cache_keys, cache_values, new_keys, new_values, prefix_len):
    cache_rows, kv_width = cache_keys.shape
    new_rows = queries.shape[0]
    heads = kv_width // HEAD_DIM
    groups = queries.shape[1] // kv_width
    key_rows = cache_rows + new_rows
    dims = (cache_rows, new_rows, STEP)
    bf16, f32 = jnp.bfloat16, jnp.float32
    shape = jax.ShapeDtypeStruct
    arguments = [
        pltpu.with_memory_space_constraint(argument, pltpu.HBM)
        for argument in (queries, cache_keys, cache_values, new_keys, new_values)
    ]

    def pack(head, pieces, after):
        return pl.pallas_call(
            functools.partial(pack_kernel, head, pieces),
            out_shape=[shape((2 * key_rows, HEAD_DIM), bf16)]
            + [shape((new_rows, groups * HEAD_DIM // pieces), bf16)] * pieces,
            in_specs=[HBM] * 5 + [ANY] * len(after),
            out_specs=[ANY] * (1 + pieces),
            scratch_shapes=[pltpu.SemaphoreType.DMA((4 + pieces,))],
            name="pack",
        )(*arguments, *after)

    def work(query, blocks, q_xor, store, state=None, after=()):
        rows = query.shape[1] // HEAD_DIM * new_rows
        pairs = key_rows * rows * len(blocks)
        out = shape((HEAD_DIM + STATS, rows), bf16) if store == "sent" else shape((HEAD_DIM + 8, rows), f32)
        carried = () if state is None else (state,)
        return pl.pallas_call(
            functools.partial(
                attend_kernel, dims, tuple(b for b, _ in blocks), q_xor, store, bool(carried), len(after)
            ),
            out_shape=out,
            in_specs=[SMEM] + [VMEM] * (1 + len(blocks) + len(carried)) + [ANY] * len(after),
            out_specs=VMEM,
            compiler_params=pltpu.CompilerParams(vmem_limit_bytes=LIMIT),
            cost_estimate=pl.CostEstimate(
                flops=4 * HEAD_DIM * pairs, bytes_accessed=1 << 20, transcendentals=pairs
            ),
            name="work",
        )(prefix_len, query, *[ref for _, ref in blocks], *carried, *after)

    def merge(own, got, columns, out=None, after=()):
        aliased = () if out is None else (out,)
        return pl.pallas_call(
            functools.partial(merge_kernel, dims, columns, bool(aliased)),
            out_shape=shape(queries.shape, bf16),
            in_specs=[VMEM] * 2 + [HBM] * len(aliased) + [ANY] * len(after),
            out_specs=HBM,
            scratch_shapes=[
                pltpu.VMEM((new_rows, columns[2] * HEAD_DIM), bf16),
                pltpu.SemaphoreType.DMA(()),
            ],
            compiler_params=pltpu.CompilerParams(vmem_limit_bytes=LIMIT),
            input_output_aliases={2: 0} if aliased else {},
            name="merge",
        )(own, got, *aliased, *after)

    half = groups // 2
    kv1, q1 = pack(1, 1, ())
    far_kv1 = traded(kv1, 2)
    kv0, q0a, q0b = pack(0, 2, (kv1,))
    far_q1 = traded(q1, 1)
    far_kv0 = traded(kv0, 1)
    far_q0 = [traded(q0a, 2), traded(q0b, 2)]
    mine1 = work(q1, [(0, kv1)], 0, "state", after=(kv0,))
    mine0 = [work(q, [(0, kv0)], 0, "state", after=(mine1,)) for q in (q0a, q0b)]
    theirs1 = work(far_q1, [(0, kv1)], 1, "state", after=tuple(mine0))
    sent1 = work(far_q1, [(2, far_kv1)], 1, "sent", state=theirs1)
    got1 = traded(sent1, 1)
    own1 = work(q1, [(2, far_kv1)], 0, "own", state=mine1, after=(sent1,))
    own0 = [
        work(q, [(1, far_kv0)], 0, "own", state=state, after=(own1,))
        for q, state in zip((q0a, q0b), mine0)
    ]
    sent0a = work(far_q0[0], [(0, kv0), (1, far_kv0)], 2, "sent", after=tuple(own0))
    got0a = traded(sent0a, 2)
    sent0b = work(far_q0[1], [(0, kv0), (1, far_kv0)], 2, "sent", after=(sent0a,))
    got0b = traded(sent0b, 2)
    out = merge(own1, got1, (groups, 0, groups), after=(sent0b,))
    out = merge(own0[0], got0a, (0, 0, half), out)
    return merge(own0[1], got0b, (half, 0, half), out)


def passed_along(value, axis, steps):
    count = lax.axis_size(axis)
    pairs = [(source, (source + steps) % count) for source in range(count)]
    return lax.ppermute(value, axis, pairs)


def allowed_for(source, query_tok, cache_rows, query_rows, length):
    key_rows = cache_rows + query_rows
    key_index = jnp.arange(key_rows, dtype=jnp.int32)
    cache_pos = source * cache_rows + key_index
    new_pos = source * query_rows + key_index - cache_rows
    return jnp.where(
        (key_index < cache_rows)[None, :],
        (cache_pos < length)[None, :],
        new_pos[None, :] <= query_tok[:, None],
    )


def softmax_block(running, query_heads, kv_block, allowed):
    old_max, old_total, old_acc = running
    scale = HEAD_DIM ** (-0.5)
    scores = (
        jnp.einsum("hrd,hkd->hrk", query_heads, kv_block[0], preferred_element_type=jnp.float32)
        * scale
    )
    scores = jnp.where(allowed[None], scores, jnp.float32(-1e30))
    new_max = jnp.maximum(old_max, jnp.max(scores, -1))
    weights = jnp.where(allowed[None], jnp.exp(scores - new_max[..., None]), jnp.float32(0.0))
    rescale = jnp.exp(old_max - new_max)
    new_total = old_total * rescale + jnp.sum(weights, -1)
    new_acc = old_acc * rescale[..., None] + jnp.einsum(
        "hrk,hkd->hrd",
        weights.astype(jnp.bfloat16),
        kv_block[1],
        preferred_element_type=jnp.float32,
    )
    return (new_max, new_total, new_acc)


def empty_state(heads, rows):
    return (
        jnp.full((heads, rows), -1e30, jnp.float32),
        jnp.zeros((heads, rows), jnp.float32),
        jnp.zeros((heads, rows, HEAD_DIM), jnp.float32),
    )


def local_ring(queries, cache_keys, cache_values, new_keys, new_values, prefix_len):
    length = prefix_len[0]
    cycle_size = lax.axis_size("ctx")
    my_index = lax.axis_index("ctx")
    cache_rows = cache_keys.shape[0]
    query_rows = queries.shape[0]
    kv_width = cache_keys.shape[1]
    kv_heads = kv_width // HEAD_DIM
    groups = queries.shape[1] // kv_width
    key_rows = cache_rows + query_rows
    stacked = jnp.stack(
        [jnp.concatenate([cache_keys, new_keys], 0), jnp.concatenate([cache_values, new_values], 0)]
    )
    kv_block = stacked.reshape(2, key_rows, kv_heads, HEAD_DIM).transpose(0, 2, 1, 3)
    query_heads = (
        queries.reshape(query_rows, kv_heads, groups, HEAD_DIM)
        .transpose(1, 0, 2, 3)
        .reshape(kv_heads, query_rows * groups, HEAD_DIM)
    )
    query_tok = my_index * query_rows + jnp.arange(query_rows * groups, dtype=jnp.int32) // groups
    running = softmax_block(
        empty_state(kv_heads, query_rows * groups),
        query_heads,
        kv_block,
        allowed_for(my_index, query_tok, cache_rows, query_rows, length),
    )

    def one_turn(turn_index, loop_state):
        running_now, held = loop_state
        held = passed_along(held, "ctx", 1)
        source = (my_index - turn_index) % cycle_size
        allowed = allowed_for(source, query_tok, cache_rows, query_rows, length)
        return (softmax_block(running_now, query_heads, held, allowed), held)

    running, held = lax.fori_loop(1, cycle_size, one_turn, (running, kv_block))
    final_max, final_total, final_acc = running
    result = final_acc / final_total[..., None]
    result = result.reshape(kv_heads, query_rows, groups, HEAD_DIM).transpose(1, 0, 2, 3)
    return result.reshape(query_rows, kv_width * groups).astype(jnp.bfloat16)


def solution(mesh):
    in_specs = (
        P(("dp", "ctx"), "tp"),
        P(("dp", "ctx"), "tp"),
        P(("dp", "ctx"), "tp"),
        P(("dp", "ctx"), "tp"),
        P(("dp", "ctx"), "tp"),
        P("dp"),
    )
    out_specs = P(("dp", "ctx"), "tp")
    local = local_four if mesh.shape["ctx"] == 4 else local_ring
    return jax.shard_map(local, mesh=mesh, in_specs=in_specs, out_specs=out_specs, check_vma=False)
```

```python
import functools

import jax
import jax.numpy as jnp
from jax import lax
from jax.experimental import pallas as pl
from jax.experimental.pallas import tpu as pltpu
from jax.sharding import PartitionSpec as P

HEAD_DIM = 128
LOW = -1e30
SLOPE = HEAD_DIM ** (-0.5) * 1.4426950408889634
STATS = 16
STEP = 4

VMEM = pl.BlockSpec(memory_space=pltpu.VMEM)
SMEM = pl.BlockSpec(memory_space=pltpu.SMEM)
HBM = pl.BlockSpec(memory_space=pltpu.HBM)
ANY = pl.BlockSpec(memory_space=pl.ANY)
LIMIT = 24 * 1024 * 1024


def attend(query, kv_ref, source, token_dev, length, cache_rows, new_rows):
    key_rows = cache_rows + new_rows
    keys = kv_ref[0:key_rows, :]
    scores = lax.dot_general(
        keys, query, (((1,), (1,)), ((), ())), preferred_element_type=jnp.float32
    )
    rows = query.shape[0]
    slot = lax.broadcasted_iota(jnp.int32, (cache_rows, rows), 0)
    cached = jnp.where(slot < length - source * cache_rows, scores[:cache_rows], LOW)
    new = lax.broadcasted_iota(jnp.int32, (new_rows, rows), 0) + source * new_rows
    token = lax.rem(
        lax.broadcasted_iota(jnp.int32, (new_rows, rows), 1), new_rows
    ) + token_dev * new_rows
    fresh = jnp.where(new <= token, scores[cache_rows:], LOW)
    scores = jnp.concatenate([cached, fresh], 0)
    top = jnp.max(scores, axis=0, keepdims=True)
    weights = jnp.exp2((scores - top) * SLOPE)
    total = jnp.sum(weights, axis=0, keepdims=True)
    values = kv_ref[key_rows : 2 * key_rows, :]
    summed = lax.dot_general(
        values,
        weights.astype(jnp.bfloat16),
        (((0,), (0,)), ((), ())),
        preferred_element_type=jnp.float32,
    )
    return top, total, summed


def joined(one, two):
    top = jnp.maximum(one[0], two[0])
    left, right = jnp.exp2((one[0] - top) * SLOPE), jnp.exp2((two[0] - top) * SLOPE)
    return top, one[1] * left + two[1] * right, one[2] * left + two[2] * right


def stacked_heads(q_ref, first, count):
    return jnp.concatenate(
        [q_ref[:, pl.ds((first + g) * HEAD_DIM, HEAD_DIM)] for g in range(count)], 0
    )


def load_state(ref, lanes):
    return (
        ref[HEAD_DIM : HEAD_DIM + 1, lanes],
        ref[HEAD_DIM + 1 : HEAD_DIM + 2, lanes],
        ref[0:HEAD_DIM, lanes],
    )


def store_state(ref, lanes, state):
    top, total, summed = state
    ref[0:HEAD_DIM, lanes] = summed
    ref[HEAD_DIM : HEAD_DIM + 1, lanes] = top
    ref[HEAD_DIM + 1 : HEAD_DIM + 2, lanes] = total


def store_own(ref, lanes, state):
    top, total, summed = state
    ref[0:HEAD_DIM, lanes] = summed * (1.0 / total)
    ref[HEAD_DIM : HEAD_DIM + 1, lanes] = top * SLOPE + jnp.log2(total)


def store_sent(ref, lanes, state):
    top, total, summed = state
    log = top * SLOPE + jnp.log2(total)
    high = log.astype(jnp.bfloat16).astype(jnp.float32)
    rest = log - high
    middle = rest.astype(jnp.bfloat16).astype(jnp.float32)
    row = lax.broadcasted_iota(jnp.int32, (STATS, log.shape[1]), 0)
    stats = jnp.where(
        row == 0, high, jnp.where(row == 1, middle, jnp.where(row == 2, rest - middle, 0.0))
    )
    ref[0:HEAD_DIM, lanes] = (summed * (1.0 / total)).astype(jnp.bfloat16)
    ref[HEAD_DIM : HEAD_DIM + STATS, lanes] = stats.astype(jnp.bfloat16)


STORES = {"state": store_state, "own": store_own, "sent": store_sent}


def attend_kernel(dims, blocks, q_xor, store, carried, after, len_ref, q_ref, *refs):
    cache_rows, new_rows, step = dims
    kv_refs, out_ref = refs[: len(blocks)], refs[-1]
    me = lax.axis_index("ctx")
    groups = q_ref.shape[1] // HEAD_DIM
    for at in range(0, groups, step):
        query = stacked_heads(q_ref, at, step)
        lanes = pl.ds(at * new_rows, step * new_rows)
        state = load_state(refs[len(blocks)], lanes) if carried else None
        for block, kv_ref in zip(blocks, kv_refs):
            ours = attend(
                query, kv_ref, me ^ block, me ^ q_xor, len_ref[0], cache_rows, new_rows
            )
            state = ours if state is None else joined(state, ours)
        STORES[store](out_ref, lanes, state)


def merge_kernel(dims, columns, aliased, own_ref, got_ref, *refs):
    cache_rows, new_rows, _ = dims
    out_ref, block_ref, sem = refs[-3:]
    first, own_first, groups = columns
    pair = HEAD_DIM // new_rows
    for at in range(0, groups, pair):
        lanes = pl.ds(at * new_rows, pair * new_rows)
        own_lanes = pl.ds((own_first + at) * new_rows, pair * new_rows)
        stats = got_ref[HEAD_DIM : HEAD_DIM + STATS, lanes].astype(jnp.float32)
        theirs = stats[0:1] + stats[1:2] + stats[2:3]
        mine = own_ref[HEAD_DIM : HEAD_DIM + 1, own_lanes]
        top = jnp.maximum(mine, theirs)
        left, right = jnp.exp2(mine - top), jnp.exp2(theirs - top)
        scale = 1.0 / (left + right)
        whole = own_ref[0:HEAD_DIM, own_lanes] * (left * scale) + got_ref[
            0:HEAD_DIM, lanes
        ].astype(jnp.float32) * (right * scale)
        turned = whole.T.astype(jnp.bfloat16)
        for g in range(pair):
            column = (at + g) * HEAD_DIM
            block_ref[:, column : column + HEAD_DIM] = turned[g * new_rows : (g + 1) * new_rows, :]
    copy = pltpu.make_async_copy(
        block_ref, out_ref.at[:, pl.ds(first * HEAD_DIM, groups * HEAD_DIM)], sem
    )
    copy.start()
    copy.wait()


def pack_kernel(head, pieces, q_ref, ck_ref, cv_ref, nk_ref, nv_ref, *rest):
    sems = rest[-1]
    kv, q_refs = rest[-2 - pieces], rest[-1 - pieces : -1]
    cache_rows, new_rows = ck_ref.shape[0], nk_ref.shape[0]
    key_rows = cache_rows + new_rows
    width = q_refs[0].shape[1]
    columns = pl.ds(head * HEAD_DIM, HEAD_DIM)
    copies = [
        (source.at[:, columns], kv.at[pl.ds(at, rows), :])
        for source, at, rows in (
            (ck_ref, 0, cache_rows),
            (nk_ref, cache_rows, new_rows),
            (cv_ref, key_rows, cache_rows),
            (nv_ref, key_rows + cache_rows, new_rows),
        )
    ] + [
        (q_ref.at[:, pl.ds((head * pieces + piece) * width, width)], q_refs[piece])
        for piece in range(pieces)
    ]
    handles = [
        pltpu.make_async_copy(source, target, sems.at[n])
        for n, (source, target) in enumerate(copies)
    ]
    for handle in handles:
        handle.start()
    for handle in handles:
        handle.wait()


def traded(value, xor):
    count = lax.axis_size("ctx")
    return lax.ppermute(value, "ctx", [(source, source ^ xor) for source in range(count)])


def local_four(queries, cache_keys, cache_values, new_keys, new_values, prefix_len):
    cache_rows, kv_width = cache_keys.shape
    new_rows = queries.shape[0]
    heads = kv_width // HEAD_DIM
    groups = queries.shape[1] // kv_width
    key_rows = cache_rows + new_rows
    dims = (cache_rows, new_rows, STEP)
    bf16, f32 = jnp.bfloat16, jnp.float32
    shape = jax.ShapeDtypeStruct
    arguments = [
        pltpu.with_memory_space_constraint(argument, pltpu.HBM)
        for argument in (queries, cache_keys, cache_values, new_keys, new_values)
    ]

    def pack(head, pieces, after):
        return pl.pallas_call(
            functools.partial(pack_kernel, head, pieces),
            out_shape=[pltpu.VMEM((2 * key_rows, HEAD_DIM), bf16)]
            + [pltpu.VMEM((new_rows, groups * HEAD_DIM // pieces), bf16)] * pieces,
            in_specs=[HBM] * 5 + [ANY] * len(after),
            out_specs=[VMEM] * (1 + pieces),
            scratch_shapes=[pltpu.SemaphoreType.DMA((4 + pieces,))],
            name="pack",
        )(*arguments, *after)

    def work(query, blocks, q_xor, store, state=None, after=()):
        rows = query.shape[1] // HEAD_DIM * new_rows
        pairs = key_rows * rows * len(blocks)
        if store == "sent":
            out = pltpu.VMEM((HEAD_DIM + STATS, rows), bf16)
        else:
            out = pltpu.VMEM((HEAD_DIM + 8, rows), f32)
        carried = () if state is None else (state,)
        return pl.pallas_call(
            functools.partial(
                attend_kernel, dims, tuple(b for b, _ in blocks), q_xor, store, bool(carried), len(after)
            ),
            out_shape=out,
            in_specs=[SMEM] + [VMEM] * (1 + len(blocks) + len(carried)) + [ANY] * len(after),
            out_specs=VMEM,
            compiler_params=pltpu.CompilerParams(vmem_limit_bytes=LIMIT),
            cost_estimate=pl.CostEstimate(
                flops=4 * HEAD_DIM * pairs * 40, bytes_accessed=1 << 20, transcendentals=pairs
            ),
            name="work",
        )(prefix_len, query, *[ref for _, ref in blocks], *carried, *after)

    def merge(own, got, columns, out=None, after=()):
        aliased = () if out is None else (out,)
        return pl.pallas_call(
            functools.partial(merge_kernel, dims, columns, bool(aliased)),
            out_shape=shape(queries.shape, bf16),
            in_specs=[VMEM] * 2 + [HBM] * len(aliased) + [ANY] * len(after),
            out_specs=HBM,
            scratch_shapes=[
                pltpu.VMEM((new_rows, columns[2] * HEAD_DIM), bf16),
                pltpu.SemaphoreType.DMA(()),
            ],
            compiler_params=pltpu.CompilerParams(vmem_limit_bytes=LIMIT),
            input_output_aliases={2: 0} if aliased else {},
            name="merge",
        )(own, got, *aliased, *after)

    kv0, q0 = pack(0, 1, ())
    far_kv0, far_q0 = traded(kv0, 1), traded(q0, 2)
    kv1, q1 = pack(1, 1, (kv0,))
    far_kv1, far_q1 = traded(kv1, 2), traded(q1, 1)
    mine0 = work(q0, [(0, kv0)], 0, "state", after=(kv1,))
    mine1 = work(q1, [(0, kv1)], 0, "state", after=(mine0,))
    theirs0 = work(far_q0, [(0, kv0)], 2, "state", after=(mine1,))
    sent0 = work(far_q0, [(1, far_kv0)], 2, "sent", state=theirs0)
    got0 = traded(sent0, 2)
    own0 = work(q0, [(1, far_kv0)], 0, "own", state=mine0, after=(sent0,))
    theirs1 = work(far_q1, [(0, kv1)], 1, "state", after=(own0,))
    sent1 = work(far_q1, [(2, far_kv1)], 1, "sent", state=theirs1)
    got1 = traded(sent1, 1)
    own1 = work(q1, [(2, far_kv1)], 0, "own", state=mine1, after=(sent1,))
    out = merge(own0, got0, (0, 0, groups), after=(own1,))
    return merge(own1, got1, (groups, 0, groups), out)


def passed_along(value, axis, steps):
    count = lax.axis_size(axis)
    pairs = [(source, (source + steps) % count) for source in range(count)]
    return lax.ppermute(value, axis, pairs)


def allowed_for(source, query_tok, cache_rows, query_rows, length):
    key_rows = cache_rows + query_rows
    key_index = jnp.arange(key_rows, dtype=jnp.int32)
    cache_pos = source * cache_rows + key_index
    new_pos = source * query_rows + key_index - cache_rows
    return jnp.where(
        (key_index < cache_rows)[None, :],
        (cache_pos < length)[None, :],
        new_pos[None, :] <= query_tok[:, None],
    )


def softmax_block(running, query_heads, kv_block, allowed):
    old_max, old_total, old_acc = running
    scale = HEAD_DIM ** (-0.5)
    scores = (
        jnp.einsum("hrd,hkd->hrk", query_heads, kv_block[0], preferred_element_type=jnp.float32)
        * scale
    )
    scores = jnp.where(allowed[None], scores, jnp.float32(-1e30))
    new_max = jnp.maximum(old_max, jnp.max(scores, -1))
    weights = jnp.where(allowed[None], jnp.exp(scores - new_max[..., None]), jnp.float32(0.0))
    rescale = jnp.exp(old_max - new_max)
    new_total = old_total * rescale + jnp.sum(weights, -1)
    new_acc = old_acc * rescale[..., None] + jnp.einsum(
        "hrk,hkd->hrd",
        weights.astype(jnp.bfloat16),
        kv_block[1],
        preferred_element_type=jnp.float32,
    )
    return (new_max, new_total, new_acc)


def empty_state(heads, rows):
    return (
        jnp.full((heads, rows), -1e30, jnp.float32),
        jnp.zeros((heads, rows), jnp.float32),
        jnp.zeros((heads, rows, HEAD_DIM), jnp.float32),
    )


def local_ring(queries, cache_keys, cache_values, new_keys, new_values, prefix_len):
    length = prefix_len[0]
    cycle_size = lax.axis_size("ctx")
    my_index = lax.axis_index("ctx")
    cache_rows = cache_keys.shape[0]
    query_rows = queries.shape[0]
    kv_width = cache_keys.shape[1]
    kv_heads = kv_width // HEAD_DIM
    groups = queries.shape[1] // kv_width
    key_rows = cache_rows + query_rows
    stacked = jnp.stack(
        [jnp.concatenate([cache_keys, new_keys], 0), jnp.concatenate([cache_values, new_values], 0)]
    )
    kv_block = stacked.reshape(2, key_rows, kv_heads, HEAD_DIM).transpose(0, 2, 1, 3)
    query_heads = (
        queries.reshape(query_rows, kv_heads, groups, HEAD_DIM)
        .transpose(1, 0, 2, 3)
        .reshape(kv_heads, query_rows * groups, HEAD_DIM)
    )
    query_tok = my_index * query_rows + jnp.arange(query_rows * groups, dtype=jnp.int32) // groups
    running = softmax_block(
        empty_state(kv_heads, query_rows * groups),
        query_heads,
        kv_block,
        allowed_for(my_index, query_tok, cache_rows, query_rows, length),
    )

    def one_turn(turn_index, loop_state):
        running_now, held = loop_state
        held = passed_along(held, "ctx", 1)
        source = (my_index - turn_index) % cycle_size
        allowed = allowed_for(source, query_tok, cache_rows, query_rows, length)
        return (softmax_block(running_now, query_heads, held, allowed), held)

    running, held = lax.fori_loop(1, cycle_size, one_turn, (running, kv_block))
    final_max, final_total, final_acc = running
    result = final_acc / final_total[..., None]
    result = result.reshape(kv_heads, query_rows, groups, HEAD_DIM).transpose(1, 0, 2, 3)
    return result.reshape(query_rows, kv_width * groups).astype(jnp.bfloat16)


def solution(mesh):
    in_specs = (
        P(("dp", "ctx"), "tp"),
        P(("dp", "ctx"), "tp"),
        P(("dp", "ctx"), "tp"),
        P(("dp", "ctx"), "tp"),
        P(("dp", "ctx"), "tp"),
        P("dp"),
    )
    out_specs = P(("dp", "ctx"), "tp")
    local = local_four if mesh.shape["ctx"] == 4 else local_ring
    return jax.shard_map(local, mesh=mesh, in_specs=in_specs, out_specs=out_specs, check_vma=False)
```

```python
import functools

import jax
import jax.numpy as jnp
from jax import lax
from jax.experimental import pallas as pl
from jax.experimental.pallas import tpu as pltpu
from jax.sharding import PartitionSpec as P

HEAD_DIM = 128
LOW = -1e30
SLOPE = HEAD_DIM ** (-0.5) * 1.4426950408889634
STEP = 8

VMEM = pl.BlockSpec(memory_space=pltpu.VMEM)
SMEM = pl.BlockSpec(memory_space=pltpu.SMEM)
HBM = pl.BlockSpec(memory_space=pltpu.HBM)
ANY = pl.BlockSpec(memory_space=pl.ANY)
LIMIT = 24 * 1024 * 1024


def attend(query, kv_ref, source, token_dev, length, cache_rows, new_rows):
    key_rows = cache_rows + new_rows
    keys = kv_ref[0:key_rows, :]
    scores = lax.dot_general(
        keys, query, (((1,), (1,)), ((), ())), preferred_element_type=jnp.float32
    )
    rows = query.shape[0]
    slot = lax.broadcasted_iota(jnp.int32, (cache_rows, rows), 0)
    cached = jnp.where(slot < length - source * cache_rows, scores[:cache_rows], LOW)
    new = lax.broadcasted_iota(jnp.int32, (new_rows, rows), 0) + source * new_rows
    token = lax.rem(
        lax.broadcasted_iota(jnp.int32, (new_rows, rows), 1), new_rows
    ) + token_dev * new_rows
    fresh = jnp.where(new <= token, scores[cache_rows:], LOW)
    scores = jnp.concatenate([cached, fresh], 0)
    top = jnp.max(scores, axis=0, keepdims=True)
    weights = jnp.exp2((scores - top) * SLOPE)
    total = jnp.sum(weights, axis=0, keepdims=True)
    values = kv_ref[key_rows : 2 * key_rows, :]
    summed = lax.dot_general(
        values,
        weights.astype(jnp.bfloat16),
        (((0,), (0,)), ((), ())),
        preferred_element_type=jnp.float32,
    )
    return top, total, summed


def joined(one, two):
    top = jnp.maximum(one[0], two[0])
    left, right = jnp.exp2((one[0] - top) * SLOPE), jnp.exp2((two[0] - top) * SLOPE)
    return top, one[1] * left + two[1] * right, one[2] * left + two[2] * right


def stacked_heads(q_ref, first, count):
    return jnp.concatenate(
        [q_ref[:, pl.ds((first + g) * HEAD_DIM, HEAD_DIM)] for g in range(count)], 0
    )


def load_state(ref, lanes):
    return (
        ref[HEAD_DIM : HEAD_DIM + 1, lanes],
        ref[HEAD_DIM + 1 : HEAD_DIM + 2, lanes],
        ref[0:HEAD_DIM, lanes],
    )


def store_state(ref, lanes, state):
    top, total, summed = state
    ref[0:HEAD_DIM, lanes] = summed
    ref[HEAD_DIM : HEAD_DIM + 1, lanes] = top
    ref[HEAD_DIM + 1 : HEAD_DIM + 2, lanes] = total


def store_own(ref, lanes, state):
    top, total, summed = state
    ref[0:HEAD_DIM, lanes] = summed * (1.0 / total)
    ref[HEAD_DIM : HEAD_DIM + 1, lanes] = top * SLOPE + jnp.log2(total)


def store_sent(ref, blocks):
    row = lax.broadcasted_iota(jnp.int32, (ref.shape[0] - len(blocks) * HEAD_DIM, HEAD_DIM), 0)
    stats = jnp.zeros(row.shape, jnp.float32)
    for n, (top, total, summed) in enumerate(blocks):
        log = top * SLOPE + jnp.log2(total)
        high = log.astype(jnp.bfloat16).astype(jnp.float32)
        rest = log - high
        middle = rest.astype(jnp.bfloat16).astype(jnp.float32)
        for i, part in enumerate((high, middle, rest - middle)):
            stats = jnp.where(row == 3 * n + i, part, stats)
        ref[n * HEAD_DIM : (n + 1) * HEAD_DIM, :] = (summed * (1.0 / total)).astype(jnp.bfloat16)
    ref[len(blocks) * HEAD_DIM :, :] = stats.astype(jnp.bfloat16)


def sent_rows(blocks):
    return blocks * HEAD_DIM + -(-3 * blocks // 16) * 16


def attend_kernel(dims, blocks, q_xor, store, carried, after, len_ref, q_ref, *refs):
    cache_rows, new_rows, step = dims
    kv_refs, out_ref = refs[: len(blocks)], refs[-1]
    me = lax.axis_index("ctx")
    groups = q_ref.shape[1] // HEAD_DIM
    sent = []
    for at in range(0, groups, step):
        query = stacked_heads(q_ref, at, step)
        lanes = pl.ds(at * new_rows, step * new_rows)
        state = load_state(refs[len(blocks)], lanes) if carried else None
        for block, kv_ref in zip(blocks, kv_refs):
            ours = attend(
                query, kv_ref, me ^ block, me ^ q_xor, len_ref[0], cache_rows, new_rows
            )
            state = ours if state is None else joined(state, ours)
        if store == "state":
            store_state(out_ref, lanes, state)
        elif store == "own":
            store_own(out_ref, lanes, state)
        else:
            for lane in range(0, step * new_rows, HEAD_DIM):
                sent.append([part[:, lane : lane + HEAD_DIM] for part in state])
    if store == "sent":
        store_sent(out_ref, sent)


def merge_kernel(dims, columns, aliased, own_ref, got_ref, *refs):
    cache_rows, new_rows, _ = dims
    out_ref, block_ref, sem = refs[-3:]
    first, own_first, groups = columns
    pair = HEAD_DIM // new_rows
    stats = got_ref[groups // pair * HEAD_DIM :, :].astype(jnp.float32)
    for at in range(0, groups, pair):
        own_lanes = pl.ds((own_first + at) * new_rows, pair * new_rows)
        n = at // pair
        theirs = sum(stats[3 * n + i : 3 * n + i + 1] for i in range(3))
        mine = own_ref[HEAD_DIM : HEAD_DIM + 1, own_lanes]
        top = jnp.maximum(mine, theirs)
        left, right = jnp.exp2(mine - top), jnp.exp2(theirs - top)
        scale = 1.0 / (left + right)
        whole = own_ref[0:HEAD_DIM, own_lanes] * (left * scale) + got_ref[
            n * HEAD_DIM : (n + 1) * HEAD_DIM, :
        ].astype(jnp.float32) * (right * scale)
        turned = whole.T.astype(jnp.bfloat16)
        for g in range(pair):
            column = (at + g) * HEAD_DIM
            block_ref[:, column : column + HEAD_DIM] = turned[g * new_rows : (g + 1) * new_rows, :]
    copy = pltpu.make_async_copy(
        block_ref, out_ref.at[:, pl.ds(first * HEAD_DIM, groups * HEAD_DIM)], sem
    )
    copy.start()
    copy.wait()


def pack_kernel(head, with_kv, with_q, *refs):
    q_ref, ck_ref, cv_ref, nk_ref, nv_ref = refs[:5]
    sems, outs = refs[-1], list(refs[-1 - with_kv - with_q : -1])
    cache_rows, new_rows = ck_ref.shape[0], nk_ref.shape[0]
    key_rows = cache_rows + new_rows
    columns = pl.ds(head * HEAD_DIM, HEAD_DIM)
    copies = []
    if with_kv:
        kv = outs.pop(0)
        for source, at, rows in (
            (ck_ref, 0, cache_rows),
            (nk_ref, cache_rows, new_rows),
            (cv_ref, key_rows, cache_rows),
            (nv_ref, key_rows + cache_rows, new_rows),
        ):
            copies.append((source.at[:, columns], kv.at[pl.ds(at, rows), :]))
    if with_q:
        width = outs[0].shape[1]
        copies.append((q_ref.at[:, pl.ds(head * width, width)], outs[0]))
    handles = [
        pltpu.make_async_copy(source, target, sems.at[n])
        for n, (source, target) in enumerate(copies)
    ]
    for handle in handles:
        handle.start()
    for handle in handles:
        handle.wait()


def traded(value, xor):
    count = lax.axis_size("ctx")
    return lax.ppermute(value, "ctx", [(source, source ^ xor) for source in range(count)])


def local_four(queries, cache_keys, cache_values, new_keys, new_values, prefix_len):
    cache_rows, kv_width = cache_keys.shape
    new_rows = queries.shape[0]
    heads = kv_width // HEAD_DIM
    groups = queries.shape[1] // kv_width
    key_rows = cache_rows + new_rows
    dims = (cache_rows, new_rows, STEP)
    bf16, f32 = jnp.bfloat16, jnp.float32
    shape = jax.ShapeDtypeStruct
    arguments = [
        pltpu.with_memory_space_constraint(argument, pltpu.HBM)
        for argument in (queries, cache_keys, cache_values, new_keys, new_values)
    ]

    def pack(head, with_kv, with_q, after):
        outs = [pltpu.VMEM((2 * key_rows, HEAD_DIM), bf16)] * with_kv
        outs += [pltpu.VMEM((new_rows, groups * HEAD_DIM), bf16)] * with_q
        return pl.pallas_call(
            functools.partial(pack_kernel, head, with_kv, with_q),
            out_shape=outs,
            in_specs=[HBM] * 5 + [ANY] * len(after),
            out_specs=[VMEM] * len(outs),
            scratch_shapes=[pltpu.SemaphoreType.DMA((4 * with_kv + with_q,))],
            name="pack",
        )(*arguments, *after)

    def work(query, blocks, q_xor, store, state=None, after=()):
        rows = query.shape[1] // HEAD_DIM * new_rows
        pairs = key_rows * rows * len(blocks)
        if store == "sent":
            out = pltpu.VMEM((sent_rows(rows // HEAD_DIM), HEAD_DIM), bf16)
        else:
            out = pltpu.VMEM((HEAD_DIM + 8, rows), f32)
        carried = () if state is None else (state,)
        return pl.pallas_call(
            functools.partial(
                attend_kernel, dims, tuple(b for b, _ in blocks), q_xor, store, bool(carried), len(after)
            ),
            out_shape=out,
            in_specs=[SMEM] + [VMEM] * (1 + len(blocks) + len(carried)) + [ANY] * len(after),
            out_specs=VMEM,
            compiler_params=pltpu.CompilerParams(vmem_limit_bytes=LIMIT),
            cost_estimate=pl.CostEstimate(
                flops=4 * HEAD_DIM * pairs * 40, bytes_accessed=1 << 20, transcendentals=pairs
            ),
            name="work",
        )(prefix_len, query, *[ref for _, ref in blocks], *carried, *after)

    def merge(own, got, columns, out=None, after=()):
        aliased = () if out is None else (out,)
        return pl.pallas_call(
            functools.partial(merge_kernel, dims, columns, bool(aliased)),
            out_shape=shape(queries.shape, bf16),
            in_specs=[VMEM] * 2 + [HBM] * len(aliased) + [ANY] * len(after),
            out_specs=HBM,
            scratch_shapes=[
                pltpu.VMEM((new_rows, columns[2] * HEAD_DIM), bf16),
                pltpu.SemaphoreType.DMA(()),
            ],
            compiler_params=pltpu.CompilerParams(vmem_limit_bytes=LIMIT),
            input_output_aliases={2: 0} if aliased else {},
            name="merge",
        )(own, got, *aliased, *after)

    kv0, q0 = pack(0, 1, 1, ())
    far_kv0, far_q0 = traded(kv0, 1), traded(q0, 2)
    (kv1,) = pack(1, 1, 0, (kv0,))
    far_kv1 = traded(kv1, 2)
    mine0 = work(q0, [(0, kv0)], 0, "state", after=(kv1,))
    (q1,) = pack(1, 0, 1, (mine0,))
    far_q1 = traded(q1, 1)
    mine1 = work(q1, [(0, kv1)], 0, "state")
    theirs0 = work(far_q0, [(0, kv0)], 2, "state", after=(mine1,))
    sent0 = work(far_q0, [(1, far_kv0)], 2, "sent", state=theirs0, after=(mine1,))
    theirs1 = work(far_q1, [(0, kv1)], 1, "state", after=(sent0,))
    got0 = traded(sent0, 2)
    sent1 = work(far_q1, [(2, far_kv1)], 1, "sent", state=theirs1)
    got1 = traded(sent1, 1)
    own0 = work(q0, [(1, far_kv0)], 0, "own", state=mine0, after=(sent1,))
    own1 = work(q1, [(2, far_kv1)], 0, "own", state=mine1, after=(own0,))
    out = merge(own0, got0, (0, 0, groups), after=(own1,))
    return merge(own1, got1, (groups, 0, groups), out)


def passed_along(value, axis, steps):
    count = lax.axis_size(axis)
    pairs = [(source, (source + steps) % count) for source in range(count)]
    return lax.ppermute(value, axis, pairs)


def allowed_for(source, query_tok, cache_rows, query_rows, length):
    key_rows = cache_rows + query_rows
    key_index = jnp.arange(key_rows, dtype=jnp.int32)
    cache_pos = source * cache_rows + key_index
    new_pos = source * query_rows + key_index - cache_rows
    return jnp.where(
        (key_index < cache_rows)[None, :],
        (cache_pos < length)[None, :],
        new_pos[None, :] <= query_tok[:, None],
    )


def softmax_block(running, query_heads, kv_block, allowed):
    old_max, old_total, old_acc = running
    scale = HEAD_DIM ** (-0.5)
    scores = (
        jnp.einsum("hrd,hkd->hrk", query_heads, kv_block[0], preferred_element_type=jnp.float32)
        * scale
    )
    scores = jnp.where(allowed[None], scores, jnp.float32(-1e30))
    new_max = jnp.maximum(old_max, jnp.max(scores, -1))
    weights = jnp.where(allowed[None], jnp.exp(scores - new_max[..., None]), jnp.float32(0.0))
    rescale = jnp.exp(old_max - new_max)
    new_total = old_total * rescale + jnp.sum(weights, -1)
    new_acc = old_acc * rescale[..., None] + jnp.einsum(
        "hrk,hkd->hrd",
        weights.astype(jnp.bfloat16),
        kv_block[1],
        preferred_element_type=jnp.float32,
    )
    return (new_max, new_total, new_acc)


def empty_state(heads, rows):
    return (
        jnp.full((heads, rows), -1e30, jnp.float32),
        jnp.zeros((heads, rows), jnp.float32),
        jnp.zeros((heads, rows, HEAD_DIM), jnp.float32),
    )


def local_ring(queries, cache_keys, cache_values, new_keys, new_values, prefix_len):
    length = prefix_len[0]
    cycle_size = lax.axis_size("ctx")
    my_index = lax.axis_index("ctx")
    cache_rows = cache_keys.shape[0]
    query_rows = queries.shape[0]
    kv_width = cache_keys.shape[1]
    kv_heads = kv_width // HEAD_DIM
    groups = queries.shape[1] // kv_width
    key_rows = cache_rows + query_rows
    stacked = jnp.stack(
        [jnp.concatenate([cache_keys, new_keys], 0), jnp.concatenate([cache_values, new_values], 0)]
    )
    kv_block = stacked.reshape(2, key_rows, kv_heads, HEAD_DIM).transpose(0, 2, 1, 3)
    query_heads = (
        queries.reshape(query_rows, kv_heads, groups, HEAD_DIM)
        .transpose(1, 0, 2, 3)
        .reshape(kv_heads, query_rows * groups, HEAD_DIM)
    )
    query_tok = my_index * query_rows + jnp.arange(query_rows * groups, dtype=jnp.int32) // groups
    running = softmax_block(
        empty_state(kv_heads, query_rows * groups),
        query_heads,
        kv_block,
        allowed_for(my_index, query_tok, cache_rows, query_rows, length),
    )

    def one_turn(turn_index, loop_state):
        running_now, held = loop_state
        held = passed_along(held, "ctx", 1)
        source = (my_index - turn_index) % cycle_size
        allowed = allowed_for(source, query_tok, cache_rows, query_rows, length)
        return (softmax_block(running_now, query_heads, held, allowed), held)

    running, held = lax.fori_loop(1, cycle_size, one_turn, (running, kv_block))
    final_max, final_total, final_acc = running
    result = final_acc / final_total[..., None]
    result = result.reshape(kv_heads, query_rows, groups, HEAD_DIM).transpose(1, 0, 2, 3)
    return result.reshape(query_rows, kv_width * groups).astype(jnp.bfloat16)


def solution(mesh):
    in_specs = (
        P(("dp", "ctx"), "tp"),
        P(("dp", "ctx"), "tp"),
        P(("dp", "ctx"), "tp"),
        P(("dp", "ctx"), "tp"),
        P(("dp", "ctx"), "tp"),
        P("dp"),
    )
    out_specs = P(("dp", "ctx"), "tp")
    local = local_four if mesh.shape["ctx"] == 4 else local_ring
    return jax.shard_map(local, mesh=mesh, in_specs=in_specs, out_specs=out_specs, check_vma=False)
```

```python
import functools

import jax
import jax.numpy as jnp
from jax import lax
from jax.experimental import pallas as pl
from jax.experimental.pallas import tpu as pltpu
from jax.sharding import PartitionSpec as P

HEAD_DIM = 128
LOW = -1e30
SLOPE = HEAD_DIM ** (-0.5) * 1.4426950408889634

VMEM = pl.BlockSpec(memory_space=pltpu.VMEM)
SMEM = pl.BlockSpec(memory_space=pltpu.SMEM)
HBM = pl.BlockSpec(memory_space=pltpu.HBM)
ANY = pl.BlockSpec(memory_space=pl.ANY)
LIMIT = 24 * 1024 * 1024


def attend(query, kv_ref, source, token_dev, length, cache_rows, new_rows):
    key_rows = cache_rows + new_rows
    keys = kv_ref[0:key_rows, :]
    scores = lax.dot_general(
        keys, query, (((1,), (1,)), ((), ())), preferred_element_type=jnp.float32
    )
    rows = query.shape[0]
    slot = lax.broadcasted_iota(jnp.int32, (cache_rows, rows), 0)
    cached = jnp.where(slot < length - source * cache_rows, scores[:cache_rows], LOW)
    new = lax.broadcasted_iota(jnp.int32, (new_rows, rows), 0) + source * new_rows
    token = lax.rem(
        lax.broadcasted_iota(jnp.int32, (new_rows, rows), 1), new_rows
    ) + token_dev * new_rows
    fresh = jnp.where(new <= token, scores[cache_rows:], LOW)
    scores = jnp.concatenate([cached, fresh], 0)
    top = jnp.max(scores, axis=0, keepdims=True)
    weights = jnp.exp2((scores - top) * SLOPE)
    total = jnp.sum(weights, axis=0, keepdims=True)
    values = kv_ref[key_rows : 2 * key_rows, :]
    summed = lax.dot_general(
        values,
        weights.astype(jnp.bfloat16),
        (((0,), (0,)), ((), ())),
        preferred_element_type=jnp.float32,
    )
    return top, total, summed


def joined(one, two):
    top = jnp.maximum(one[0], two[0])
    left, right = jnp.exp2((one[0] - top) * SLOPE), jnp.exp2((two[0] - top) * SLOPE)
    return top, one[1] * left + two[1] * right, one[2] * left + two[2] * right


def stacked_heads(q_ref, first, count):
    return jnp.concatenate(
        [q_ref[:, pl.ds((first + g) * HEAD_DIM, HEAD_DIM)] for g in range(count)], 0
    )


def load_state(ref, lanes):
    return (
        ref[HEAD_DIM : HEAD_DIM + 1, lanes],
        ref[HEAD_DIM + 1 : HEAD_DIM + 2, lanes],
        ref[0:HEAD_DIM, lanes],
    )


def store_state(ref, lanes, state):
    top, total, summed = state
    ref[0:HEAD_DIM, lanes] = summed
    ref[HEAD_DIM : HEAD_DIM + 1, lanes] = top
    ref[HEAD_DIM + 1 : HEAD_DIM + 2, lanes] = total


def store_own(ref, lanes, state):
    top, total, summed = state
    ref[0:HEAD_DIM, lanes] = summed * (1.0 / total)
    ref[HEAD_DIM : HEAD_DIM + 1, lanes] = top * SLOPE + jnp.log2(total)


def store_sent(ref, blocks):
    row = lax.broadcasted_iota(jnp.int32, (ref.shape[0] - len(blocks) * HEAD_DIM, HEAD_DIM), 0)
    stats = jnp.zeros(row.shape, jnp.float32)
    for n, (top, total, summed) in enumerate(blocks):
        log = top * SLOPE + jnp.log2(total)
        high = log.astype(jnp.bfloat16).astype(jnp.float32)
        rest = log - high
        middle = rest.astype(jnp.bfloat16).astype(jnp.float32)
        for i, part in enumerate((high, middle, rest - middle)):
            stats = jnp.where(row == 3 * n + i, part, stats)
        ref[n * HEAD_DIM : (n + 1) * HEAD_DIM, :] = (summed * (1.0 / total)).astype(jnp.bfloat16)
    ref[len(blocks) * HEAD_DIM :, :] = stats.astype(jnp.bfloat16)


def sent_rows(blocks):
    return blocks * HEAD_DIM + -(-3 * blocks // 16) * 16


def attend_kernel(dims, blocks, q_xor, store, carried, len_ref, q_ref, *refs):
    cache_rows, new_rows, step = dims
    kv_refs, out_ref = refs[: len(blocks)], refs[-1]
    me = lax.axis_index("ctx")
    groups = q_ref.shape[1] // HEAD_DIM
    sent = []
    for at in range(0, groups, step):
        query = stacked_heads(q_ref, at, step)
        lanes = pl.ds(at * new_rows, step * new_rows)
        state = load_state(refs[len(blocks)], lanes) if carried else None
        for block, kv_ref in zip(blocks, kv_refs):
            ours = attend(
                query, kv_ref, me ^ block, me ^ q_xor, len_ref[0], cache_rows, new_rows
            )
            state = ours if state is None else joined(state, ours)
        if store == "state":
            store_state(out_ref, lanes, state)
        elif store == "own":
            store_own(out_ref, lanes, state)
        else:
            for lane in range(0, step * new_rows, HEAD_DIM):
                sent.append([part[:, lane : lane + HEAD_DIM] for part in state])
    if store == "sent":
        store_sent(out_ref, sent)


def merge_kernel(dims, columns, own_ref, got_ref, *refs):
    cache_rows, new_rows, _ = dims
    out_ref, block_ref, sem = refs[-3:]
    first, own_first, groups = columns
    pair = HEAD_DIM // new_rows
    stats = got_ref[groups // pair * HEAD_DIM :, :].astype(jnp.float32)
    for at in range(0, groups, pair):
        own_lanes = pl.ds((own_first + at) * new_rows, pair * new_rows)
        n = at // pair
        theirs = sum(stats[3 * n + i : 3 * n + i + 1] for i in range(3))
        mine = own_ref[HEAD_DIM : HEAD_DIM + 1, own_lanes]
        top = jnp.maximum(mine, theirs)
        left, right = jnp.exp2(mine - top), jnp.exp2(theirs - top)
        scale = 1.0 / (left + right)
        whole = own_ref[0:HEAD_DIM, own_lanes] * (left * scale) + got_ref[
            n * HEAD_DIM : (n + 1) * HEAD_DIM, :
        ].astype(jnp.float32) * (right * scale)
        turned = whole.T.astype(jnp.bfloat16)
        for g in range(pair):
            column = (at + g) * HEAD_DIM
            block_ref[:, column : column + HEAD_DIM] = turned[g * new_rows : (g + 1) * new_rows, :]
    copy = pltpu.make_async_copy(
        block_ref, out_ref.at[:, pl.ds(first * HEAD_DIM, groups * HEAD_DIM)], sem
    )
    copy.start()
    copy.wait()


def pack_kernel(head, with_kv, with_q, *refs):
    q_ref, ck_ref, cv_ref, nk_ref, nv_ref = refs[:5]
    sems, outs = refs[-1], list(refs[-1 - with_kv - with_q : -1])
    cache_rows, new_rows = ck_ref.shape[0], nk_ref.shape[0]
    key_rows = cache_rows + new_rows
    columns = pl.ds(head * HEAD_DIM, HEAD_DIM)
    copies = []
    if with_kv:
        kv = outs.pop(0)
        for source, at, rows in (
            (ck_ref, 0, cache_rows),
            (nk_ref, cache_rows, new_rows),
            (cv_ref, key_rows, cache_rows),
            (nv_ref, key_rows + cache_rows, new_rows),
        ):
            copies.append((source.at[:, columns], kv.at[pl.ds(at, rows), :]))
    if with_q:
        width = outs[0].shape[1]
        copies.append((q_ref.at[:, pl.ds(head * width, width)], outs[0]))
    handles = [
        pltpu.make_async_copy(source, target, sems.at[n])
        for n, (source, target) in enumerate(copies)
    ]
    for handle in handles:
        handle.start()
    for handle in handles:
        handle.wait()


def traded(value, xor):
    count = lax.axis_size("ctx")
    return lax.ppermute(value, "ctx", [(source, source ^ xor) for source in range(count)])


def local_four(queries, cache_keys, cache_values, new_keys, new_values, prefix_len):
    cache_rows, kv_width = cache_keys.shape
    new_rows = queries.shape[0]
    heads = kv_width // HEAD_DIM
    groups = queries.shape[1] // kv_width
    key_rows = cache_rows + new_rows
    dims = (cache_rows, new_rows, groups)
    bf16, f32 = jnp.bfloat16, jnp.float32
    shape = jax.ShapeDtypeStruct
    arguments = [
        pltpu.with_memory_space_constraint(argument, pltpu.HBM)
        for argument in (queries, cache_keys, cache_values, new_keys, new_values)
    ]

    def pack(head, with_kv, with_q, after):
        outs = [pltpu.VMEM((2 * key_rows, HEAD_DIM), bf16)] * with_kv
        outs += [pltpu.VMEM((new_rows, groups * HEAD_DIM), bf16)] * with_q
        return pl.pallas_call(
            functools.partial(pack_kernel, head, with_kv, with_q),
            out_shape=outs,
            in_specs=[HBM] * 5 + [ANY] * len(after),
            out_specs=[VMEM] * len(outs),
            scratch_shapes=[pltpu.SemaphoreType.DMA((4 * with_kv + with_q,))],
            compiler_params=pltpu.CompilerParams(vmem_limit_bytes=2 * 1024 * 1024),
            name="pack",
        )(*arguments, *after)

    def work(query, blocks, q_xor, store, state=None, after=()):
        rows = query.shape[1] // HEAD_DIM * new_rows
        pairs = key_rows * rows * len(blocks)
        if store == "sent":
            out = pltpu.VMEM((sent_rows(rows // HEAD_DIM), HEAD_DIM), bf16)
        else:
            out = pltpu.VMEM((HEAD_DIM + 8, rows), f32)
        carried = () if state is None else (state,)
        return pl.pallas_call(
            functools.partial(
                attend_kernel, dims, tuple(b for b, _ in blocks), q_xor, store, bool(carried)
            ),
            out_shape=out,
            in_specs=[SMEM] + [VMEM] * (1 + len(blocks) + len(carried)) + [ANY] * len(after),
            out_specs=VMEM,
            compiler_params=pltpu.CompilerParams(vmem_limit_bytes=LIMIT),
            cost_estimate=pl.CostEstimate(
                flops=4 * HEAD_DIM * pairs * 40, bytes_accessed=1 << 20, transcendentals=pairs
            ),
            name="work",
        )(prefix_len, query, *[ref for _, ref in blocks], *carried, *after)

    def merge(own, got, columns, out=None, after=()):
        aliased = () if out is None else (out,)
        return pl.pallas_call(
            functools.partial(merge_kernel, dims, columns),
            out_shape=shape(queries.shape, bf16),
            in_specs=[VMEM] * 2 + [HBM] * len(aliased) + [ANY] * len(after),
            out_specs=HBM,
            scratch_shapes=[
                pltpu.VMEM((new_rows, columns[2] * HEAD_DIM), bf16),
                pltpu.SemaphoreType.DMA(()),
            ],
            compiler_params=pltpu.CompilerParams(vmem_limit_bytes=LIMIT),
            input_output_aliases={2: 0} if aliased else {},
            name="merge",
        )(own, got, *aliased, *after)

    kv0, q0 = pack(0, 1, 1, ())
    far_kv0, far_q0 = traded(kv0, 1), traded(q0, 2)
    kv1, q1 = pack(1, 1, 1, (kv0,))
    far_kv1 = traded(kv1, 3)
    mine0 = work(q0, [(0, kv0)], 0, "state", after=(kv1,))
    sent_q1, mine0 = lax.optimization_barrier((q1, mine0))
    far_q1 = traded(sent_q1, 1)
    mine1 = work(q1, [(0, kv1)], 0, "state", after=(mine0,))
    theirs0 = work(far_q0, [(0, kv0)], 2, "state", after=(mine1,))
    sent0 = work(far_q0, [(1, far_kv0)], 2, "sent", state=theirs0, after=(mine1,))
    got0 = traded(sent0, 2)
    theirs1 = work(far_q1, [(0, kv1)], 1, "state", after=(sent0,))
    sent1 = work(far_q1, [(3, far_kv1)], 1, "sent", state=theirs1)
    got1 = traded(sent1, 1)
    own0 = work(q0, [(1, far_kv0)], 0, "own", state=mine0, after=(sent1,))
    own1 = work(q1, [(3, far_kv1)], 0, "own", state=mine1, after=(own0,))
    out = merge(own0, got0, (0, 0, groups), after=(own1,))
    return merge(own1, got1, (groups, 0, groups), out)


def passed_along(value, axis, steps):
    count = lax.axis_size(axis)
    pairs = [(source, (source + steps) % count) for source in range(count)]
    return lax.ppermute(value, axis, pairs)


def allowed_for(source, query_tok, cache_rows, query_rows, length):
    key_rows = cache_rows + query_rows
    key_index = jnp.arange(key_rows, dtype=jnp.int32)
    cache_pos = source * cache_rows + key_index
    new_pos = source * query_rows + key_index - cache_rows
    return jnp.where(
        (key_index < cache_rows)[None, :],
        (cache_pos < length)[None, :],
        new_pos[None, :] <= query_tok[:, None],
    )


def softmax_block(running, query_heads, kv_block, allowed):
    old_max, old_total, old_acc = running
    scale = HEAD_DIM ** (-0.5)
    scores = (
        jnp.einsum("hrd,hkd->hrk", query_heads, kv_block[0], preferred_element_type=jnp.float32)
        * scale
    )
    scores = jnp.where(allowed[None], scores, jnp.float32(-1e30))
    new_max = jnp.maximum(old_max, jnp.max(scores, -1))
    weights = jnp.where(allowed[None], jnp.exp(scores - new_max[..., None]), jnp.float32(0.0))
    rescale = jnp.exp(old_max - new_max)
    new_total = old_total * rescale + jnp.sum(weights, -1)
    new_acc = old_acc * rescale[..., None] + jnp.einsum(
        "hrk,hkd->hrd",
        weights.astype(jnp.bfloat16),
        kv_block[1],
        preferred_element_type=jnp.float32,
    )
    return (new_max, new_total, new_acc)


def empty_state(heads, rows):
    return (
        jnp.full((heads, rows), -1e30, jnp.float32),
        jnp.zeros((heads, rows), jnp.float32),
        jnp.zeros((heads, rows, HEAD_DIM), jnp.float32),
    )


def local_ring(queries, cache_keys, cache_values, new_keys, new_values, prefix_len):
    length = prefix_len[0]
    cycle_size = lax.axis_size("ctx")
    my_index = lax.axis_index("ctx")
    cache_rows = cache_keys.shape[0]
    query_rows = queries.shape[0]
    kv_width = cache_keys.shape[1]
    kv_heads = kv_width // HEAD_DIM
    groups = queries.shape[1] // kv_width
    key_rows = cache_rows + query_rows
    stacked = jnp.stack(
        [jnp.concatenate([cache_keys, new_keys], 0), jnp.concatenate([cache_values, new_values], 0)]
    )
    kv_block = stacked.reshape(2, key_rows, kv_heads, HEAD_DIM).transpose(0, 2, 1, 3)
    query_heads = (
        queries.reshape(query_rows, kv_heads, groups, HEAD_DIM)
        .transpose(1, 0, 2, 3)
        .reshape(kv_heads, query_rows * groups, HEAD_DIM)
    )
    query_tok = my_index * query_rows + jnp.arange(query_rows * groups, dtype=jnp.int32) // groups
    running = softmax_block(
        empty_state(kv_heads, query_rows * groups),
        query_heads,
        kv_block,
        allowed_for(my_index, query_tok, cache_rows, query_rows, length),
    )

    def one_turn(turn_index, loop_state):
        running_now, held = loop_state
        held = passed_along(held, "ctx", 1)
        source = (my_index - turn_index) % cycle_size
        allowed = allowed_for(source, query_tok, cache_rows, query_rows, length)
        return (softmax_block(running_now, query_heads, held, allowed), held)

    running, held = lax.fori_loop(1, cycle_size, one_turn, (running, kv_block))
    final_max, final_total, final_acc = running
    result = final_acc / final_total[..., None]
    result = result.reshape(kv_heads, query_rows, groups, HEAD_DIM).transpose(1, 0, 2, 3)
    return result.reshape(query_rows, kv_width * groups).astype(jnp.bfloat16)


def local(*arguments):
    if lax.axis_size("ctx") == 4 and arguments[1].shape[1] == 2 * HEAD_DIM:
        return local_four(*arguments)
    return local_ring(*arguments)


def solution(mesh):
    in_specs = (
        P(("dp", "ctx"), "tp"),
        P(("dp", "ctx"), "tp"),
        P(("dp", "ctx"), "tp"),
        P(("dp", "ctx"), "tp"),
        P(("dp", "ctx"), "tp"),
        P("dp"),
    )
    out_specs = P(("dp", "ctx"), "tp")
    return jax.shard_map(local, mesh=mesh, in_specs=in_specs, out_specs=out_specs, check_vma=False)
```

```python
import functools

import jax
import jax.numpy as jnp
from jax import lax
from jax.experimental import pallas as pl
from jax.experimental.pallas import tpu as pltpu
from jax.sharding import PartitionSpec as P

HEAD_DIM = 128
LOW = -1e30
SLOPE = HEAD_DIM ** (-0.5) * 1.4426950408889634

VMEM = pl.BlockSpec(memory_space=pltpu.VMEM)
SMEM = pl.BlockSpec(memory_space=pltpu.SMEM)
HBM = pl.BlockSpec(memory_space=pltpu.HBM)
ANY = pl.BlockSpec(memory_space=pl.ANY)
LIMIT = 24 * 1024 * 1024


def attend(query, kv_refs, source, token_dev, length, cache_rows, new_rows):
    key_rows = cache_rows + new_rows
    if len(kv_refs) == 1:
        keys, values = kv_refs[0][0:key_rows, :], kv_refs[0][key_rows : 2 * key_rows, :]
    else:
        old, fresh_rows = kv_refs
        keys = jnp.concatenate([old[0:cache_rows, :], fresh_rows[0:new_rows, :]], 0)
        values = jnp.concatenate([old[cache_rows:, :], fresh_rows[new_rows:, :]], 0)
    scores = lax.dot_general(
        keys, query, (((1,), (1,)), ((), ())), preferred_element_type=jnp.float32
    )
    rows = query.shape[0]
    slot = lax.broadcasted_iota(jnp.int32, (cache_rows, rows), 0)
    cached = jnp.where(slot < length - source * cache_rows, scores[:cache_rows], LOW)
    new = lax.broadcasted_iota(jnp.int32, (new_rows, rows), 0) + source * new_rows
    token = lax.rem(
        lax.broadcasted_iota(jnp.int32, (new_rows, rows), 1), new_rows
    ) + token_dev * new_rows
    fresh = jnp.where(new <= token, scores[cache_rows:], LOW)
    scores = jnp.concatenate([cached, fresh], 0)
    top = jnp.max(scores, axis=0, keepdims=True)
    weights = jnp.exp2((scores - top) * SLOPE)
    total = jnp.sum(weights, axis=0, keepdims=True)
    summed = lax.dot_general(
        values,
        weights.astype(jnp.bfloat16),
        (((0,), (0,)), ((), ())),
        preferred_element_type=jnp.float32,
    )
    return top, total, summed


def joined(one, two):
    top = jnp.maximum(one[0], two[0])
    left, right = jnp.exp2((one[0] - top) * SLOPE), jnp.exp2((two[0] - top) * SLOPE)
    return top, one[1] * left + two[1] * right, one[2] * left + two[2] * right


def stacked_heads(q_ref, first, count):
    return jnp.concatenate(
        [q_ref[:, pl.ds((first + g) * HEAD_DIM, HEAD_DIM)] for g in range(count)], 0
    )


def load_state(ref, lanes):
    return (
        ref[HEAD_DIM : HEAD_DIM + 1, lanes],
        ref[HEAD_DIM + 1 : HEAD_DIM + 2, lanes],
        ref[0:HEAD_DIM, lanes],
    )


def store_state(ref, lanes, state):
    top, total, summed = state
    ref[0:HEAD_DIM, lanes] = summed
    ref[HEAD_DIM : HEAD_DIM + 1, lanes] = top
    ref[HEAD_DIM + 1 : HEAD_DIM + 2, lanes] = total


def store_own(ref, lanes, state):
    top, total, summed = state
    ref[0:HEAD_DIM, lanes] = summed * (1.0 / total)
    ref[HEAD_DIM : HEAD_DIM + 1, lanes] = top * SLOPE + jnp.log2(total)


def store_sent(ref, blocks):
    row = lax.broadcasted_iota(jnp.int32, (ref.shape[0] - len(blocks) * HEAD_DIM, HEAD_DIM), 0)
    stats = jnp.zeros(row.shape, jnp.float32)
    for n, (top, total, summed) in enumerate(blocks):
        log = top * SLOPE + jnp.log2(total)
        high = log.astype(jnp.bfloat16).astype(jnp.float32)
        rest = log - high
        middle = rest.astype(jnp.bfloat16).astype(jnp.float32)
        for i, part in enumerate((high, middle, rest - middle)):
            stats = jnp.where(row == 3 * n + i, part, stats)
        ref[n * HEAD_DIM : (n + 1) * HEAD_DIM, :] = (summed * (1.0 / total)).astype(jnp.bfloat16)
    ref[len(blocks) * HEAD_DIM :, :] = stats.astype(jnp.bfloat16)


def sent_rows(blocks):
    return blocks * HEAD_DIM + -(-3 * blocks // 16) * 16


def attend_kernel(dims, blocks, q_xor, store, carried, len_ref, q_ref, *refs):
    cache_rows, new_rows, step = dims
    out_ref, kv_refs = refs[-1], []
    for _, count in blocks:
        kv_refs.append(refs[:count])
        refs = refs[count:]
    me = lax.axis_index("ctx")
    groups = q_ref.shape[1] // HEAD_DIM
    sent = []
    for at in range(0, groups, step):
        query = stacked_heads(q_ref, at, step)
        lanes = pl.ds(at * new_rows, step * new_rows)
        state = load_state(refs[0], lanes) if carried else None
        for (block, _), kv_ref in zip(blocks, kv_refs):
            ours = attend(
                query, kv_ref, me ^ block, me ^ q_xor, len_ref[0], cache_rows, new_rows
            )
            state = ours if state is None else joined(state, ours)
        if store == "state":
            store_state(out_ref, lanes, state)
        elif store == "own":
            store_own(out_ref, lanes, state)
        else:
            for lane in range(0, step * new_rows, HEAD_DIM):
                sent.append([part[:, lane : lane + HEAD_DIM] for part in state])
    if store == "sent":
        store_sent(out_ref, sent)


def merge_kernel(dims, columns, own_ref, got_ref, *refs):
    cache_rows, new_rows, _ = dims
    out_ref, block_ref, sem = refs[-3:]
    first, own_first, groups = columns
    pair = HEAD_DIM // new_rows
    stats = got_ref[groups // pair * HEAD_DIM :, :].astype(jnp.float32)
    for at in range(0, groups, pair):
        own_lanes = pl.ds((own_first + at) * new_rows, pair * new_rows)
        n = at // pair
        theirs = sum(stats[3 * n + i : 3 * n + i + 1] for i in range(3))
        mine = own_ref[HEAD_DIM : HEAD_DIM + 1, own_lanes]
        top = jnp.maximum(mine, theirs)
        left, right = jnp.exp2(mine - top), jnp.exp2(theirs - top)
        scale = 1.0 / (left + right)
        whole = own_ref[0:HEAD_DIM, own_lanes] * (left * scale) + got_ref[
            n * HEAD_DIM : (n + 1) * HEAD_DIM, :
        ].astype(jnp.float32) * (right * scale)
        turned = whole.T.astype(jnp.bfloat16)
        for g in range(pair):
            column = (at + g) * HEAD_DIM
            block_ref[:, column : column + HEAD_DIM] = turned[g * new_rows : (g + 1) * new_rows, :]
    copy = pltpu.make_async_copy(
        block_ref, out_ref.at[:, pl.ds(first * HEAD_DIM, groups * HEAD_DIM)], sem
    )
    copy.start()
    copy.wait()


def pack_kernel(head, apart, q_ref, ck_ref, cv_ref, nk_ref, nv_ref, *refs):
    sems, outs = refs[-1], refs[-3 - apart : -1]
    cache_rows, new_rows = ck_ref.shape[0], nk_ref.shape[0]
    key_rows = cache_rows + new_rows
    columns = pl.ds(head * HEAD_DIM, HEAD_DIM)
    if apart:
        places = ((0, 0), (0, cache_rows), (1, 0), (1, new_rows))
    else:
        places = ((0, 0), (0, key_rows), (0, cache_rows), (0, key_rows + cache_rows))
    copies = [
        (source.at[:, columns], outs[array].at[pl.ds(at, source.shape[0]), :])
        for source, (array, at) in zip((ck_ref, cv_ref, nk_ref, nv_ref), places)
    ]
    width = outs[-1].shape[1]
    copies.append((q_ref.at[:, pl.ds(head * width, width)], outs[-1]))
    handles = [
        pltpu.make_async_copy(source, target, sems.at[n])
        for n, (source, target) in enumerate(copies)
    ]
    for handle in handles:
        handle.start()
    for handle in handles:
        handle.wait()


def traded(value, xor, onward=False):
    pairs = [(source, source ^ xor) for source in range(lax.axis_size("ctx"))]
    return lax.ppermute(value, "ctx", [(a, b) for a, b in pairs if a < b or not onward])


def local_four(queries, cache_keys, cache_values, new_keys, new_values, prefix_len):
    cache_rows, kv_width = cache_keys.shape
    new_rows = queries.shape[0]
    heads = kv_width // HEAD_DIM
    groups = queries.shape[1] // kv_width
    key_rows = cache_rows + new_rows
    dims = (cache_rows, new_rows, groups)
    bf16, f32 = jnp.bfloat16, jnp.float32
    shape = jax.ShapeDtypeStruct
    arguments = [
        pltpu.with_memory_space_constraint(argument, pltpu.HBM)
        for argument in (queries, cache_keys, cache_values, new_keys, new_values)
    ]

    def pack(head, apart, after):
        rows = [2 * cache_rows, 2 * new_rows] if apart else [2 * key_rows]
        return pl.pallas_call(
            functools.partial(pack_kernel, head, apart),
            out_shape=[pltpu.VMEM((n, HEAD_DIM), bf16) for n in rows]
            + [pltpu.VMEM((new_rows, groups * HEAD_DIM), bf16)],
            in_specs=[HBM] * 5 + [ANY] * len(after),
            out_specs=[VMEM] * (len(rows) + 1),
            scratch_shapes=[pltpu.SemaphoreType.DMA((5,))],
            compiler_params=pltpu.CompilerParams(vmem_limit_bytes=2 * 1024 * 1024),
            name="pack",
        )(*arguments, *after)

    def work(query, blocks, q_xor, store, state=None, after=()):
        rows = query.shape[1] // HEAD_DIM * new_rows
        pairs = key_rows * rows * len(blocks)
        if store == "sent":
            out = pltpu.VMEM((sent_rows(rows // HEAD_DIM), HEAD_DIM), bf16)
        else:
            out = pltpu.VMEM((HEAD_DIM + 8, rows), f32)
        carried = () if state is None else (state,)
        refs = [r for _, ref in blocks for r in ref]
        return pl.pallas_call(
            functools.partial(
                attend_kernel, dims, tuple((b, len(ref)) for b, ref in blocks), q_xor, store, bool(carried)
            ),
            out_shape=out,
            in_specs=[SMEM] + [VMEM] * (1 + len(refs) + len(carried)) + [ANY] * len(after),
            out_specs=VMEM,
            compiler_params=pltpu.CompilerParams(vmem_limit_bytes=LIMIT),
            cost_estimate=pl.CostEstimate(
                flops=4 * HEAD_DIM * pairs * 40, bytes_accessed=1 << 20, transcendentals=pairs
            ),
            name="work",
        )(prefix_len, query, *refs, *carried, *after)

    def merge(own, got, columns, out=None, after=()):
        aliased = () if out is None else (out,)
        return pl.pallas_call(
            functools.partial(merge_kernel, dims, columns),
            out_shape=shape(queries.shape, bf16),
            in_specs=[VMEM] * 2 + [HBM] * len(aliased) + [ANY] * len(after),
            out_specs=HBM,
            scratch_shapes=[
                pltpu.VMEM((new_rows, columns[2] * HEAD_DIM), bf16),
                pltpu.SemaphoreType.DMA(()),
            ],
            compiler_params=pltpu.CompilerParams(vmem_limit_bytes=LIMIT),
            input_output_aliases={2: 0} if aliased else {},
            name="merge",
        )(own, got, *aliased, *after)

    kv0, q0 = pack(0, 0, ())
    far_kv0, far_q0 = traded(kv0, 1), traded(q0, 2)
    old1, new1, q1 = pack(1, 1, (kv0,))
    far_old1 = traded(old1, 3)
    mine0 = work(q0, [(0, (kv0,))], 0, "state", after=(old1,))
    sent_q1, mine0 = lax.optimization_barrier((q1, mine0))
    far_q1 = traded(sent_q1, 1)
    mine1 = work(q1, [(0, (old1, new1))], 0, "state", after=(mine0,))
    sent_new1, mine1 = lax.optimization_barrier((new1, mine1))
    far_new1 = traded(sent_new1, 3, True)
    theirs0 = work(far_q0, [(0, (kv0,))], 2, "state", after=(mine1,))
    sent0 = work(far_q0, [(1, (far_kv0,))], 2, "sent", state=theirs0, after=(mine1,))
    got0 = traded(sent0, 2)
    theirs1 = work(far_q1, [(0, (old1, new1))], 1, "state", after=(sent0,))
    sent1 = work(far_q1, [(3, (far_old1, far_new1))], 1, "sent", state=theirs1)
    got1 = traded(sent1, 1)
    own0 = work(q0, [(1, (far_kv0,))], 0, "own", state=mine0, after=(sent1,))
    own1 = work(q1, [(3, (far_old1, far_new1))], 0, "own", state=mine1, after=(own0,))
    out = merge(own0, got0, (0, 0, groups), after=(own1,))
    return merge(own1, got1, (groups, 0, groups), out)


def passed_along(value, axis, steps):
    count = lax.axis_size(axis)
    pairs = [(source, (source + steps) % count) for source in range(count)]
    return lax.ppermute(value, axis, pairs)


def allowed_for(source, query_tok, cache_rows, query_rows, length):
    key_rows = cache_rows + query_rows
    key_index = jnp.arange(key_rows, dtype=jnp.int32)
    cache_pos = source * cache_rows + key_index
    new_pos = source * query_rows + key_index - cache_rows
    return jnp.where(
        (key_index < cache_rows)[None, :],
        (cache_pos < length)[None, :],
        new_pos[None, :] <= query_tok[:, None],
    )


def softmax_block(running, query_heads, kv_block, allowed):
    old_max, old_total, old_acc = running
    scale = HEAD_DIM ** (-0.5)
    scores = (
        jnp.einsum("hrd,hkd->hrk", query_heads, kv_block[0], preferred_element_type=jnp.float32)
        * scale
    )
    scores = jnp.where(allowed[None], scores, jnp.float32(-1e30))
    new_max = jnp.maximum(old_max, jnp.max(scores, -1))
    weights = jnp.where(allowed[None], jnp.exp(scores - new_max[..., None]), jnp.float32(0.0))
    rescale = jnp.exp(old_max - new_max)
    new_total = old_total * rescale + jnp.sum(weights, -1)
    new_acc = old_acc * rescale[..., None] + jnp.einsum(
        "hrk,hkd->hrd",
        weights.astype(jnp.bfloat16),
        kv_block[1],
        preferred_element_type=jnp.float32,
    )
    return (new_max, new_total, new_acc)


def empty_state(heads, rows):
    return (
        jnp.full((heads, rows), -1e30, jnp.float32),
        jnp.zeros((heads, rows), jnp.float32),
        jnp.zeros((heads, rows, HEAD_DIM), jnp.float32),
    )


def local_ring(queries, cache_keys, cache_values, new_keys, new_values, prefix_len):
    length = prefix_len[0]
    cycle_size = lax.axis_size("ctx")
    my_index = lax.axis_index("ctx")
    cache_rows = cache_keys.shape[0]
    query_rows = queries.shape[0]
    kv_width = cache_keys.shape[1]
    kv_heads = kv_width // HEAD_DIM
    groups = queries.shape[1] // kv_width
    key_rows = cache_rows + query_rows
    stacked = jnp.stack(
        [jnp.concatenate([cache_keys, new_keys], 0), jnp.concatenate([cache_values, new_values], 0)]
    )
    kv_block = stacked.reshape(2, key_rows, kv_heads, HEAD_DIM).transpose(0, 2, 1, 3)
    query_heads = (
        queries.reshape(query_rows, kv_heads, groups, HEAD_DIM)
        .transpose(1, 0, 2, 3)
        .reshape(kv_heads, query_rows * groups, HEAD_DIM)
    )
    query_tok = my_index * query_rows + jnp.arange(query_rows * groups, dtype=jnp.int32) // groups
    running = softmax_block(
        empty_state(kv_heads, query_rows * groups),
        query_heads,
        kv_block,
        allowed_for(my_index, query_tok, cache_rows, query_rows, length),
    )

    def one_turn(turn_index, loop_state):
        running_now, held = loop_state
        held = passed_along(held, "ctx", 1)
        source = (my_index - turn_index) % cycle_size
        allowed = allowed_for(source, query_tok, cache_rows, query_rows, length)
        return (softmax_block(running_now, query_heads, held, allowed), held)

    running, held = lax.fori_loop(1, cycle_size, one_turn, (running, kv_block))
    final_max, final_total, final_acc = running
    result = final_acc / final_total[..., None]
    result = result.reshape(kv_heads, query_rows, groups, HEAD_DIM).transpose(1, 0, 2, 3)
    return result.reshape(query_rows, kv_width * groups).astype(jnp.bfloat16)


def local(*arguments):
    if lax.axis_size("ctx") == 4 and arguments[1].shape[1] == 2 * HEAD_DIM:
        return local_four(*arguments)
    return local_ring(*arguments)


def solution(mesh):
    in_specs = (
        P(("dp", "ctx"), "tp"),
        P(("dp", "ctx"), "tp"),
        P(("dp", "ctx"), "tp"),
        P(("dp", "ctx"), "tp"),
        P(("dp", "ctx"), "tp"),
        P("dp"),
    )
    out_specs = P(("dp", "ctx"), "tp")
    return jax.shard_map(local, mesh=mesh, in_specs=in_specs, out_specs=out_specs, check_vma=False)
```

```python
import functools

import jax
import jax.numpy as jnp
from jax import lax
from jax.experimental import pallas as pl
from jax.experimental.pallas import tpu as pltpu
from jax.sharding import PartitionSpec as P

HEAD_DIM = 128
LOW = -1e30
SLOPE = HEAD_DIM ** (-0.5) * 1.4426950408889634

VMEM = pl.BlockSpec(memory_space=pltpu.VMEM)
SMEM = pl.BlockSpec(memory_space=pltpu.SMEM)
HBM = pl.BlockSpec(memory_space=pltpu.HBM)
ANY = pl.BlockSpec(memory_space=pl.ANY)
LIMIT = 24 * 1024 * 1024


def attend(query, kv_refs, source, token_dev, length, cache_rows, new_rows):
    key_rows = cache_rows + new_rows
    if len(kv_refs) == 1:
        keys, values = kv_refs[0][0:key_rows, :], kv_refs[0][key_rows : 2 * key_rows, :]
    else:
        old, fresh_rows = kv_refs
        keys = jnp.concatenate([old[0:cache_rows, :], fresh_rows[0:new_rows, :]], 0)
        values = jnp.concatenate([old[cache_rows:, :], fresh_rows[new_rows:, :]], 0)
    scores = lax.dot_general(
        keys, query, (((1,), (1,)), ((), ())), preferred_element_type=jnp.float32
    )
    rows = query.shape[0]
    slot = lax.broadcasted_iota(jnp.int32, (cache_rows, rows), 0)
    cached = jnp.where(slot < length - source * cache_rows, scores[:cache_rows], LOW)
    new = lax.broadcasted_iota(jnp.int32, (new_rows, rows), 0) + source * new_rows
    token = lax.rem(
        lax.broadcasted_iota(jnp.int32, (new_rows, rows), 1), new_rows
    ) + token_dev * new_rows
    fresh = jnp.where(new <= token, scores[cache_rows:], LOW)
    scores = jnp.concatenate([cached, fresh], 0)
    top = jnp.max(scores, axis=0, keepdims=True)
    weights = jnp.exp2((scores - top) * SLOPE)
    total = jnp.sum(weights, axis=0, keepdims=True)
    summed = lax.dot_general(
        values,
        weights.astype(jnp.bfloat16),
        (((0,), (0,)), ((), ())),
        preferred_element_type=jnp.float32,
    )
    return top, total, summed


def joined(one, two):
    top = jnp.maximum(one[0], two[0])
    left, right = jnp.exp2((one[0] - top) * SLOPE), jnp.exp2((two[0] - top) * SLOPE)
    return top, one[1] * left + two[1] * right, one[2] * left + two[2] * right


def stacked_heads(q_ref, first, count):
    return jnp.concatenate(
        [q_ref[:, pl.ds((first + g) * HEAD_DIM, HEAD_DIM)] for g in range(count)], 0
    )


def load_state(ref, lanes):
    return (
        ref[HEAD_DIM : HEAD_DIM + 1, lanes],
        ref[HEAD_DIM + 1 : HEAD_DIM + 2, lanes],
        ref[0:HEAD_DIM, lanes],
    )


def store_state(ref, lanes, state):
    top, total, summed = state
    ref[0:HEAD_DIM, lanes] = summed
    ref[HEAD_DIM : HEAD_DIM + 1, lanes] = top
    ref[HEAD_DIM + 1 : HEAD_DIM + 2, lanes] = total


def store_own(ref, lanes, state):
    top, total, summed = state
    ref[0:HEAD_DIM, lanes] = summed * (1.0 / total)
    ref[HEAD_DIM : HEAD_DIM + 1, lanes] = top * SLOPE + jnp.log2(total)


def store_sent(ref, blocks):
    row = lax.broadcasted_iota(jnp.int32, (ref.shape[0] - len(blocks) * HEAD_DIM, HEAD_DIM), 0)
    stats = jnp.zeros(row.shape, jnp.float32)
    for n, (top, total, summed) in enumerate(blocks):
        log = top * SLOPE + jnp.log2(total)
        high = log.astype(jnp.bfloat16).astype(jnp.float32)
        rest = log - high
        middle = rest.astype(jnp.bfloat16).astype(jnp.float32)
        for i, part in enumerate((high, middle, rest - middle)):
            stats = jnp.where(row == 3 * n + i, part, stats)
        ref[n * HEAD_DIM : (n + 1) * HEAD_DIM, :] = (summed * (1.0 / total)).astype(jnp.bfloat16)
    ref[len(blocks) * HEAD_DIM :, :] = stats.astype(jnp.bfloat16)


def sent_rows(blocks):
    return blocks * HEAD_DIM + -(-3 * blocks // 16) * 16


def attend_kernel(dims, blocks, q_xor, store, carried, len_ref, q_ref, *refs):
    cache_rows, new_rows, step = dims
    out_ref, kv_refs = refs[-1], []
    for _, count in blocks:
        kv_refs.append(refs[:count])
        refs = refs[count:]
    me = lax.axis_index("ctx")
    groups = q_ref.shape[1] // HEAD_DIM
    sent = []
    for at in range(0, groups, step):
        query = stacked_heads(q_ref, at, step)
        lanes = pl.ds(at * new_rows, step * new_rows)
        state = load_state(refs[0], lanes) if carried else None
        for (block, _), kv_ref in zip(blocks, kv_refs):
            ours = attend(
                query, kv_ref, me ^ block, me ^ q_xor, len_ref[0], cache_rows, new_rows
            )
            state = ours if state is None else joined(state, ours)
        if store == "state":
            store_state(out_ref, lanes, state)
        elif store == "own":
            store_own(out_ref, lanes, state)
        else:
            for lane in range(0, step * new_rows, HEAD_DIM):
                sent.append([part[:, lane : lane + HEAD_DIM] for part in state])
    if store == "sent":
        store_sent(out_ref, sent)


def merge_kernel(dims, columns, own_ref, got_ref, *refs):
    cache_rows, new_rows, _ = dims
    out_ref, block_ref, sem = refs[-3:]
    first, own_first, groups = columns
    pair = HEAD_DIM // new_rows
    stats = got_ref[groups // pair * HEAD_DIM :, :].astype(jnp.float32)
    for at in range(0, groups, pair):
        own_lanes = pl.ds((own_first + at) * new_rows, pair * new_rows)
        n = at // pair
        theirs = sum(stats[3 * n + i : 3 * n + i + 1] for i in range(3))
        mine = own_ref[HEAD_DIM : HEAD_DIM + 1, own_lanes]
        top = jnp.maximum(mine, theirs)
        left, right = jnp.exp2(mine - top), jnp.exp2(theirs - top)
        scale = 1.0 / (left + right)
        whole = own_ref[0:HEAD_DIM, own_lanes] * (left * scale) + got_ref[
            n * HEAD_DIM : (n + 1) * HEAD_DIM, :
        ].astype(jnp.float32) * (right * scale)
        turned = whole.T.astype(jnp.bfloat16)
        for g in range(pair):
            column = (at + g) * HEAD_DIM
            block_ref[:, column : column + HEAD_DIM] = turned[g * new_rows : (g + 1) * new_rows, :]
    copy = pltpu.make_async_copy(
        block_ref, out_ref.at[:, pl.ds(first * HEAD_DIM, groups * HEAD_DIM)], sem
    )
    copy.start()
    copy.wait()


def pack_kernel(head, apart, q_ref, ck_ref, cv_ref, nk_ref, nv_ref, *refs):
    sems, outs = refs[-1], refs[-3 - apart : -1]
    cache_rows, new_rows = ck_ref.shape[0], nk_ref.shape[0]
    key_rows = cache_rows + new_rows
    columns = pl.ds(head * HEAD_DIM, HEAD_DIM)
    if apart:
        places = ((0, 0), (0, cache_rows), (1, 0), (1, new_rows))
    else:
        places = ((0, 0), (0, key_rows), (0, cache_rows), (0, key_rows + cache_rows))
    copies = [
        (source.at[:, columns], outs[array].at[pl.ds(at, source.shape[0]), :])
        for source, (array, at) in zip((ck_ref, cv_ref, nk_ref, nv_ref), places)
    ]
    width = outs[-1].shape[1]
    copies.append((q_ref.at[:, pl.ds(head * width, width)], outs[-1]))
    handles = [
        pltpu.make_async_copy(source, target, sems.at[n])
        for n, (source, target) in enumerate(copies)
    ]
    for handle in handles:
        handle.start()
    for handle in handles:
        handle.wait()


def traded(value, xor, onward=False):
    pairs = [(source, source ^ xor) for source in range(lax.axis_size("ctx"))]
    return lax.ppermute(value, "ctx", [(a, b) for a, b in pairs if a < b or not onward])


def local_four(queries, cache_keys, cache_values, new_keys, new_values, prefix_len):
    cache_rows, kv_width = cache_keys.shape
    new_rows = queries.shape[0]
    heads = kv_width // HEAD_DIM
    groups = queries.shape[1] // kv_width
    key_rows = cache_rows + new_rows
    dims = (cache_rows, new_rows, groups)
    bf16, f32 = jnp.bfloat16, jnp.float32
    shape = jax.ShapeDtypeStruct
    arguments = [
        pltpu.with_memory_space_constraint(argument, pltpu.HBM)
        for argument in (queries, cache_keys, cache_values, new_keys, new_values)
    ]

    def pack(head, apart, after):
        rows = [2 * cache_rows, 2 * new_rows] if apart else [2 * key_rows]
        return pl.pallas_call(
            functools.partial(pack_kernel, head, apart),
            out_shape=[pltpu.VMEM((n, HEAD_DIM), bf16) for n in rows]
            + [pltpu.VMEM((new_rows, groups * HEAD_DIM), bf16)],
            in_specs=[HBM] * 5 + [ANY] * len(after),
            out_specs=[VMEM] * (len(rows) + 1),
            scratch_shapes=[pltpu.SemaphoreType.DMA((5,))],
            compiler_params=pltpu.CompilerParams(vmem_limit_bytes=2 * 1024 * 1024),
            name="pack",
        )(*arguments, *after)

    def work(query, blocks, q_xor, store, state=None, after=()):
        rows = query.shape[1] // HEAD_DIM * new_rows
        pairs = key_rows * rows * len(blocks)
        if store == "sent":
            out = pltpu.VMEM((sent_rows(rows // HEAD_DIM), HEAD_DIM), bf16)
        else:
            out = pltpu.VMEM((HEAD_DIM + 8, rows), f32)
        carried = () if state is None else (state,)
        refs = [r for _, ref in blocks for r in ref]
        return pl.pallas_call(
            functools.partial(
                attend_kernel, dims, tuple((b, len(ref)) for b, ref in blocks), q_xor, store, bool(carried)
            ),
            out_shape=out,
            in_specs=[SMEM] + [VMEM] * (1 + len(refs) + len(carried)) + [ANY] * len(after),
            out_specs=VMEM,
            compiler_params=pltpu.CompilerParams(vmem_limit_bytes=LIMIT),
            cost_estimate=pl.CostEstimate(
                flops=4 * HEAD_DIM * pairs * 40, bytes_accessed=1 << 20, transcendentals=pairs
            ),
            name="work",
        )(prefix_len, query, *refs, *carried, *after)

    def merge(own, got, columns, out=None, after=()):
        aliased = () if out is None else (out,)
        return pl.pallas_call(
            functools.partial(merge_kernel, dims, columns),
            out_shape=shape(queries.shape, bf16),
            in_specs=[VMEM] * 2 + [HBM] * len(aliased) + [ANY] * len(after),
            out_specs=HBM,
            scratch_shapes=[
                pltpu.VMEM((new_rows, columns[2] * HEAD_DIM), bf16),
                pltpu.SemaphoreType.DMA(()),
            ],
            compiler_params=pltpu.CompilerParams(vmem_limit_bytes=LIMIT),
            input_output_aliases={2: 0} if aliased else {},
            name="merge",
        )(own, got, *aliased, *after)

    kv0, q0 = pack(0, 0, ())
    far_kv0, far_q0 = traded(kv0, 1), traded(q0, 2)
    old1, new1, q1 = pack(1, 1, (kv0,))
    far_old1 = traded(old1, 2)
    mine0 = work(q0, [(0, (kv0,))], 0, "state", after=(old1,))
    mine1 = work(q1, [(0, (old1, new1))], 0, "state", after=(mine0,))
    sent_q1, mine1 = lax.optimization_barrier((q1, mine1))
    far_q1 = traded(sent_q1, 1)
    theirs0 = work(far_q0, [(0, (kv0,))], 2, "state", after=(mine1,))
    sent_new1, theirs0 = lax.optimization_barrier((new1, theirs0))
    far_new1 = traded(sent_new1, 2, True)
    sent0 = work(far_q0, [(1, (far_kv0,))], 2, "sent", state=theirs0, after=(mine1,))
    got0 = traded(sent0, 2)
    sent1 = work(far_q1, [(0, (old1, new1)), (2, (far_old1, far_new1))], 1, "sent", after=(sent0,))
    got1 = traded(sent1, 1)
    own0 = work(q0, [(1, (far_kv0,))], 0, "own", state=mine0, after=(sent1,))
    own1 = work(q1, [(2, (far_old1, far_new1))], 0, "own", state=mine1, after=(own0,))
    out = merge(own0, got0, (0, 0, groups), after=(own1,))
    return merge(own1, got1, (groups, 0, groups), out)


def passed_along(value, axis, steps):
    count = lax.axis_size(axis)
    pairs = [(source, (source + steps) % count) for source in range(count)]
    return lax.ppermute(value, axis, pairs)


def allowed_for(source, query_tok, cache_rows, query_rows, length):
    key_rows = cache_rows + query_rows
    key_index = jnp.arange(key_rows, dtype=jnp.int32)
    cache_pos = source * cache_rows + key_index
    new_pos = source * query_rows + key_index - cache_rows
    return jnp.where(
        (key_index < cache_rows)[None, :],
        (cache_pos < length)[None, :],
        new_pos[None, :] <= query_tok[:, None],
    )


def softmax_block(running, query_heads, kv_block, allowed):
    old_max, old_total, old_acc = running
    scale = HEAD_DIM ** (-0.5)
    scores = (
        jnp.einsum("hrd,hkd->hrk", query_heads, kv_block[0], preferred_element_type=jnp.float32)
        * scale
    )
    scores = jnp.where(allowed[None], scores, jnp.float32(-1e30))
    new_max = jnp.maximum(old_max, jnp.max(scores, -1))
    weights = jnp.where(allowed[None], jnp.exp(scores - new_max[..., None]), jnp.float32(0.0))
    rescale = jnp.exp(old_max - new_max)
    new_total = old_total * rescale + jnp.sum(weights, -1)
    new_acc = old_acc * rescale[..., None] + jnp.einsum(
        "hrk,hkd->hrd",
        weights.astype(jnp.bfloat16),
        kv_block[1],
        preferred_element_type=jnp.float32,
    )
    return (new_max, new_total, new_acc)


def empty_state(heads, rows):
    return (
        jnp.full((heads, rows), -1e30, jnp.float32),
        jnp.zeros((heads, rows), jnp.float32),
        jnp.zeros((heads, rows, HEAD_DIM), jnp.float32),
    )


def local_ring(queries, cache_keys, cache_values, new_keys, new_values, prefix_len):
    length = prefix_len[0]
    cycle_size = lax.axis_size("ctx")
    my_index = lax.axis_index("ctx")
    cache_rows = cache_keys.shape[0]
    query_rows = queries.shape[0]
    kv_width = cache_keys.shape[1]
    kv_heads = kv_width // HEAD_DIM
    groups = queries.shape[1] // kv_width
    key_rows = cache_rows + query_rows
    stacked = jnp.stack(
        [jnp.concatenate([cache_keys, new_keys], 0), jnp.concatenate([cache_values, new_values], 0)]
    )
    kv_block = stacked.reshape(2, key_rows, kv_heads, HEAD_DIM).transpose(0, 2, 1, 3)
    query_heads = (
        queries.reshape(query_rows, kv_heads, groups, HEAD_DIM)
        .transpose(1, 0, 2, 3)
        .reshape(kv_heads, query_rows * groups, HEAD_DIM)
    )
    query_tok = my_index * query_rows + jnp.arange(query_rows * groups, dtype=jnp.int32) // groups
    running = softmax_block(
        empty_state(kv_heads, query_rows * groups),
        query_heads,
        kv_block,
        allowed_for(my_index, query_tok, cache_rows, query_rows, length),
    )

    def one_turn(turn_index, loop_state):
        running_now, held = loop_state
        held = passed_along(held, "ctx", 1)
        source = (my_index - turn_index) % cycle_size
        allowed = allowed_for(source, query_tok, cache_rows, query_rows, length)
        return (softmax_block(running_now, query_heads, held, allowed), held)

    running, held = lax.fori_loop(1, cycle_size, one_turn, (running, kv_block))
    final_max, final_total, final_acc = running
    result = final_acc / final_total[..., None]
    result = result.reshape(kv_heads, query_rows, groups, HEAD_DIM).transpose(1, 0, 2, 3)
    return result.reshape(query_rows, kv_width * groups).astype(jnp.bfloat16)


def local(*arguments):
    if lax.axis_size("ctx") == 4 and arguments[1].shape[1] == 2 * HEAD_DIM:
        return local_four(*arguments)
    return local_ring(*arguments)


def solution(mesh):
    in_specs = (
        P(("dp", "ctx"), "tp"),
        P(("dp", "ctx"), "tp"),
        P(("dp", "ctx"), "tp"),
        P(("dp", "ctx"), "tp"),
        P(("dp", "ctx"), "tp"),
        P("dp"),
    )
    out_specs = P(("dp", "ctx"), "tp")
    return jax.shard_map(local, mesh=mesh, in_specs=in_specs, out_specs=out_specs, check_vma=False)
```

```python
import functools

import jax
import jax.numpy as jnp
from jax import lax
from jax.experimental import pallas as pl
from jax.experimental.pallas import tpu as pltpu
from jax.sharding import PartitionSpec as P

HEAD_DIM = 128
LOW = -1e30
SLOPE = HEAD_DIM ** (-0.5) * 1.4426950408889634

VMEM = pl.BlockSpec(memory_space=pltpu.VMEM)
SMEM = pl.BlockSpec(memory_space=pltpu.SMEM)
HBM = pl.BlockSpec(memory_space=pltpu.HBM)
ANY = pl.BlockSpec(memory_space=pl.ANY)
LIMIT = 24 * 1024 * 1024


def attend(query, kv_refs, source, token_dev, length, cache_rows, new_rows):
    key_rows = cache_rows + new_rows
    if len(kv_refs) == 1:
        keys, values = kv_refs[0][0:key_rows, :], kv_refs[0][key_rows : 2 * key_rows, :]
    else:
        old, fresh_rows = kv_refs
        keys = jnp.concatenate([old[0:cache_rows, :], fresh_rows[0:new_rows, :]], 0)
        values = jnp.concatenate([old[cache_rows:, :], fresh_rows[new_rows:, :]], 0)
    scores = lax.dot_general(
        keys, query, (((1,), (1,)), ((), ())), preferred_element_type=jnp.float32
    )
    rows = query.shape[0]
    slot = lax.broadcasted_iota(jnp.int32, (cache_rows, rows), 0)
    cached = jnp.where(slot < length - source * cache_rows, scores[:cache_rows], LOW)
    new = lax.broadcasted_iota(jnp.int32, (new_rows, rows), 0) + source * new_rows
    token = lax.rem(
        lax.broadcasted_iota(jnp.int32, (new_rows, rows), 1), new_rows
    ) + token_dev * new_rows
    fresh = jnp.where(new <= token, scores[cache_rows:], LOW)
    scores = jnp.concatenate([cached, fresh], 0)
    top = jnp.max(scores, axis=0, keepdims=True)
    weights = jnp.exp2((scores - top) * SLOPE)
    total = jnp.sum(weights, axis=0, keepdims=True)
    summed = lax.dot_general(
        values,
        weights.astype(jnp.bfloat16),
        (((0,), (0,)), ((), ())),
        preferred_element_type=jnp.float32,
    )
    return top, total, summed


def joined(one, two):
    top = jnp.maximum(one[0], two[0])
    left, right = jnp.exp2((one[0] - top) * SLOPE), jnp.exp2((two[0] - top) * SLOPE)
    return top, one[1] * left + two[1] * right, one[2] * left + two[2] * right


def stacked_heads(q_ref, first, count):
    return jnp.concatenate(
        [q_ref[:, pl.ds((first + g) * HEAD_DIM, HEAD_DIM)] for g in range(count)], 0
    )


def load_state(ref, lanes):
    return (
        ref[HEAD_DIM : HEAD_DIM + 1, lanes],
        ref[HEAD_DIM + 1 : HEAD_DIM + 2, lanes],
        ref[0:HEAD_DIM, lanes],
    )


def store_state(ref, lanes, state):
    top, total, summed = state
    ref[0:HEAD_DIM, lanes] = summed
    ref[HEAD_DIM : HEAD_DIM + 1, lanes] = top
    ref[HEAD_DIM + 1 : HEAD_DIM + 2, lanes] = total


def store_own(ref, lanes, state):
    top, total, summed = state
    ref[0:HEAD_DIM, lanes] = summed * (1.0 / total)
    ref[HEAD_DIM : HEAD_DIM + 1, lanes] = top * SLOPE + jnp.log2(total)


def store_sent(ref, blocks):
    row = lax.broadcasted_iota(jnp.int32, (ref.shape[0] - len(blocks) * HEAD_DIM, HEAD_DIM), 0)
    stats = jnp.zeros(row.shape, jnp.float32)
    for n, (top, total, summed) in enumerate(blocks):
        log = top * SLOPE + jnp.log2(total)
        high = log.astype(jnp.bfloat16).astype(jnp.float32)
        rest = log - high
        middle = rest.astype(jnp.bfloat16).astype(jnp.float32)
        for i, part in enumerate((high, middle, rest - middle)):
            stats = jnp.where(row == 3 * n + i, part, stats)
        ref[n * HEAD_DIM : (n + 1) * HEAD_DIM, :] = (summed * (1.0 / total)).astype(jnp.bfloat16)
    ref[len(blocks) * HEAD_DIM :, :] = stats.astype(jnp.bfloat16)


def sent_rows(blocks):
    return blocks * HEAD_DIM + -(-3 * blocks // 16) * 16


def attend_kernel(dims, blocks, q_xor, store, carried, len_ref, q_ref, *refs):
    cache_rows, new_rows, step = dims
    out_ref, kv_refs = refs[-1], []
    for _, count in blocks:
        kv_refs.append(refs[:count])
        refs = refs[count:]
    me = lax.axis_index("ctx")
    groups = q_ref.shape[1] // HEAD_DIM
    sent = []
    for at in range(0, groups, step):
        query = stacked_heads(q_ref, at, step)
        lanes = pl.ds(at * new_rows, step * new_rows)
        state = load_state(refs[0], lanes) if carried else None
        for (block, _), kv_ref in zip(blocks, kv_refs):
            ours = attend(
                query, kv_ref, me ^ block, me ^ q_xor, len_ref[0], cache_rows, new_rows
            )
            state = ours if state is None else joined(state, ours)
        if store == "state":
            store_state(out_ref, lanes, state)
        elif store == "own":
            store_own(out_ref, lanes, state)
        else:
            for lane in range(0, step * new_rows, HEAD_DIM):
                sent.append([part[:, lane : lane + HEAD_DIM] for part in state])
    if store == "sent":
        store_sent(out_ref, sent)


def merge_kernel(dims, columns, own_ref, got_ref, *refs):
    cache_rows, new_rows, _ = dims
    out_ref, block_ref, sem = refs[-3:]
    first, own_first, groups = columns
    pair = HEAD_DIM // new_rows
    stats = got_ref[groups // pair * HEAD_DIM :, :].astype(jnp.float32)
    for at in range(0, groups, pair):
        own_lanes = pl.ds((own_first + at) * new_rows, pair * new_rows)
        n = at // pair
        theirs = sum(stats[3 * n + i : 3 * n + i + 1] for i in range(3))
        mine = own_ref[HEAD_DIM : HEAD_DIM + 1, own_lanes]
        top = jnp.maximum(mine, theirs)
        left, right = jnp.exp2(mine - top), jnp.exp2(theirs - top)
        scale = 1.0 / (left + right)
        whole = own_ref[0:HEAD_DIM, own_lanes] * (left * scale) + got_ref[
            n * HEAD_DIM : (n + 1) * HEAD_DIM, :
        ].astype(jnp.float32) * (right * scale)
        turned = whole.T.astype(jnp.bfloat16)
        for g in range(pair):
            column = (at + g) * HEAD_DIM
            block_ref[:, column : column + HEAD_DIM] = turned[g * new_rows : (g + 1) * new_rows, :]
    copy = pltpu.make_async_copy(
        block_ref, out_ref.at[:, pl.ds(first * HEAD_DIM, groups * HEAD_DIM)], sem
    )
    copy.start()
    copy.wait()


def pack_kernel(head, apart, q_ref, ck_ref, cv_ref, nk_ref, nv_ref, *refs):
    sems, outs = refs[-1], refs[-3 - apart : -1]
    cache_rows, new_rows = ck_ref.shape[0], nk_ref.shape[0]
    key_rows = cache_rows + new_rows
    columns = pl.ds(head * HEAD_DIM, HEAD_DIM)
    if apart:
        places = ((0, 0), (0, cache_rows), (1, 0), (1, new_rows))
    else:
        places = ((0, 0), (0, key_rows), (0, cache_rows), (0, key_rows + cache_rows))
    copies = [
        (source.at[:, columns], outs[array].at[pl.ds(at, source.shape[0]), :])
        for source, (array, at) in zip((ck_ref, cv_ref, nk_ref, nv_ref), places)
    ]
    width = outs[-1].shape[1]
    copies.append((q_ref.at[:, pl.ds(head * width, width)], outs[-1]))
    handles = [
        pltpu.make_async_copy(source, target, sems.at[n])
        for n, (source, target) in enumerate(copies)
    ]
    for handle in handles:
        handle.start()
    for handle in handles:
        handle.wait()


def traded(value, xor, onward=False):
    pairs = [(source, source ^ xor) for source in range(lax.axis_size("ctx"))]
    return lax.ppermute(value, "ctx", [(a, b) for a, b in pairs if a < b or not onward])


def local_four(queries, cache_keys, cache_values, new_keys, new_values, prefix_len):
    cache_rows, kv_width = cache_keys.shape
    new_rows = queries.shape[0]
    heads = kv_width // HEAD_DIM
    groups = queries.shape[1] // kv_width
    key_rows = cache_rows + new_rows
    dims = (cache_rows, new_rows, groups)
    bf16, f32 = jnp.bfloat16, jnp.float32
    shape = jax.ShapeDtypeStruct
    arguments = [
        pltpu.with_memory_space_constraint(argument, pltpu.HBM)
        for argument in (queries, cache_keys, cache_values, new_keys, new_values)
    ]

    def pack(head, apart, after):
        rows = [2 * cache_rows, 2 * new_rows] if apart else [2 * key_rows]
        return pl.pallas_call(
            functools.partial(pack_kernel, head, apart),
            out_shape=[pltpu.VMEM((n, HEAD_DIM), bf16) for n in rows]
            + [pltpu.VMEM((new_rows, groups * HEAD_DIM), bf16)],
            in_specs=[HBM] * 5 + [ANY] * len(after),
            out_specs=[VMEM] * (len(rows) + 1),
            scratch_shapes=[pltpu.SemaphoreType.DMA((5,))],
            compiler_params=pltpu.CompilerParams(vmem_limit_bytes=2 * 1024 * 1024),
            name="pack",
        )(*arguments, *after)

    def work(query, blocks, q_xor, store, state=None, after=()):
        rows = query.shape[1] // HEAD_DIM * new_rows
        pairs = key_rows * rows * len(blocks)
        if store == "sent":
            out = pltpu.VMEM((sent_rows(rows // HEAD_DIM), HEAD_DIM), bf16)
        else:
            out = pltpu.VMEM((HEAD_DIM + 8, rows), f32)
        carried = () if state is None else (state,)
        refs = [r for _, ref in blocks for r in ref]
        return pl.pallas_call(
            functools.partial(
                attend_kernel, dims, tuple((b, len(ref)) for b, ref in blocks), q_xor, store, bool(carried)
            ),
            out_shape=out,
            in_specs=[SMEM] + [VMEM] * (1 + len(refs) + len(carried)) + [ANY] * len(after),
            out_specs=VMEM,
            compiler_params=pltpu.CompilerParams(vmem_limit_bytes=LIMIT),
            cost_estimate=pl.CostEstimate(
                flops=4 * HEAD_DIM * pairs * 40, bytes_accessed=1 << 20, transcendentals=pairs
            ),
            name="work",
        )(prefix_len, query, *refs, *carried, *after)

    def merge(own, got, columns, out=None, after=()):
        aliased = () if out is None else (out,)
        return pl.pallas_call(
            functools.partial(merge_kernel, dims, columns),
            out_shape=shape(queries.shape, bf16),
            in_specs=[VMEM] * 2 + [HBM] * len(aliased) + [ANY] * len(after),
            out_specs=HBM,
            scratch_shapes=[
                pltpu.VMEM((new_rows, columns[2] * HEAD_DIM), bf16),
                pltpu.SemaphoreType.DMA(()),
            ],
            compiler_params=pltpu.CompilerParams(vmem_limit_bytes=LIMIT),
            input_output_aliases={2: 0} if aliased else {},
            name="merge",
        )(own, got, *aliased, *after)

    kv0, q0 = pack(0, 0, ())
    far_kv0, far_q0 = traded(kv0, 1), traded(q0, 2)
    old1, new1, q1 = pack(1, 1, (kv0,))
    far_old1 = traded(old1, 2)
    mine0 = work(q0, [(0, (kv0,))], 0, "state", after=(old1,))
    mine1 = work(q1, [(0, (old1, new1))], 0, "state", after=(mine0,))
    sent_q1, mine1 = lax.optimization_barrier((q1, mine1))
    far_q1 = traded(sent_q1, 1)
    theirs0 = work(far_q0, [(0, (kv0,))], 2, "state", after=(mine1,))
    sent_new1, theirs0 = lax.optimization_barrier((new1, theirs0))
    far_new1 = traded(sent_new1, 2, True)
    sent0 = work(far_q0, [(1, (far_kv0,))], 2, "sent", state=theirs0, after=(mine1,))
    got0 = traded(sent0, 2)
    own0 = work(q0, [(1, (far_kv0,))], 0, "own", state=mine0, after=(sent0,))
    sent1 = work(far_q1, [(0, (old1, new1)), (2, (far_old1, far_new1))], 1, "sent", after=(own0,))
    got1 = traded(sent1, 1)
    own1 = work(q1, [(2, (far_old1, far_new1))], 0, "own", state=mine1, after=(sent1,))
    out = merge(own0, got0, (0, 0, groups), after=(own1,))
    return merge(own1, got1, (groups, 0, groups), out)


def passed_along(value, axis, steps):
    count = lax.axis_size(axis)
    pairs = [(source, (source + steps) % count) for source in range(count)]
    return lax.ppermute(value, axis, pairs)


def allowed_for(source, query_tok, cache_rows, query_rows, length):
    key_rows = cache_rows + query_rows
    key_index = jnp.arange(key_rows, dtype=jnp.int32)
    cache_pos = source * cache_rows + key_index
    new_pos = source * query_rows + key_index - cache_rows
    return jnp.where(
        (key_index < cache_rows)[None, :],
        (cache_pos < length)[None, :],
        new_pos[None, :] <= query_tok[:, None],
    )


def softmax_block(running, query_heads, kv_block, allowed):
    old_max, old_total, old_acc = running
    scale = HEAD_DIM ** (-0.5)
    scores = (
        jnp.einsum("hrd,hkd->hrk", query_heads, kv_block[0], preferred_element_type=jnp.float32)
        * scale
    )
    scores = jnp.where(allowed[None], scores, jnp.float32(-1e30))
    new_max = jnp.maximum(old_max, jnp.max(scores, -1))
    weights = jnp.where(allowed[None], jnp.exp(scores - new_max[..., None]), jnp.float32(0.0))
    rescale = jnp.exp(old_max - new_max)
    new_total = old_total * rescale + jnp.sum(weights, -1)
    new_acc = old_acc * rescale[..., None] + jnp.einsum(
        "hrk,hkd->hrd",
        weights.astype(jnp.bfloat16),
        kv_block[1],
        preferred_element_type=jnp.float32,
    )
    return (new_max, new_total, new_acc)


def empty_state(heads, rows):
    return (
        jnp.full((heads, rows), -1e30, jnp.float32),
        jnp.zeros((heads, rows), jnp.float32),
        jnp.zeros((heads, rows, HEAD_DIM), jnp.float32),
    )


def local_ring(queries, cache_keys, cache_values, new_keys, new_values, prefix_len):
    length = prefix_len[0]
    cycle_size = lax.axis_size("ctx")
    my_index = lax.axis_index("ctx")
    cache_rows = cache_keys.shape[0]
    query_rows = queries.shape[0]
    kv_width = cache_keys.shape[1]
    kv_heads = kv_width // HEAD_DIM
    groups = queries.shape[1] // kv_width
    key_rows = cache_rows + query_rows
    stacked = jnp.stack(
        [jnp.concatenate([cache_keys, new_keys], 0), jnp.concatenate([cache_values, new_values], 0)]
    )
    kv_block = stacked.reshape(2, key_rows, kv_heads, HEAD_DIM).transpose(0, 2, 1, 3)
    query_heads = (
        queries.reshape(query_rows, kv_heads, groups, HEAD_DIM)
        .transpose(1, 0, 2, 3)
        .reshape(kv_heads, query_rows * groups, HEAD_DIM)
    )
    query_tok = my_index * query_rows + jnp.arange(query_rows * groups, dtype=jnp.int32) // groups
    running = softmax_block(
        empty_state(kv_heads, query_rows * groups),
        query_heads,
        kv_block,
        allowed_for(my_index, query_tok, cache_rows, query_rows, length),
    )

    def one_turn(turn_index, loop_state):
        running_now, held = loop_state
        held = passed_along(held, "ctx", 1)
        source = (my_index - turn_index) % cycle_size
        allowed = allowed_for(source, query_tok, cache_rows, query_rows, length)
        return (softmax_block(running_now, query_heads, held, allowed), held)

    running, held = lax.fori_loop(1, cycle_size, one_turn, (running, kv_block))
    final_max, final_total, final_acc = running
    result = final_acc / final_total[..., None]
    result = result.reshape(kv_heads, query_rows, groups, HEAD_DIM).transpose(1, 0, 2, 3)
    return result.reshape(query_rows, kv_width * groups).astype(jnp.bfloat16)


def local(*arguments):
    if lax.axis_size("ctx") == 4 and arguments[1].shape[1] == 2 * HEAD_DIM:
        return local_four(*arguments)
    return local_ring(*arguments)


def solution(mesh):
    in_specs = (
        P(("dp", "ctx"), "tp"),
        P(("dp", "ctx"), "tp"),
        P(("dp", "ctx"), "tp"),
        P(("dp", "ctx"), "tp"),
        P(("dp", "ctx"), "tp"),
        P("dp"),
    )
    out_specs = P(("dp", "ctx"), "tp")
    return jax.shard_map(local, mesh=mesh, in_specs=in_specs, out_specs=out_specs, check_vma=False)
```

```python
import functools

import jax
import jax.numpy as jnp
from jax import lax
from jax.experimental import pallas as pl
from jax.experimental.pallas import tpu as pltpu
from jax.sharding import PartitionSpec as P

HEAD_DIM = 128
LOW = -1e30
SLOPE = HEAD_DIM ** (-0.5) * 1.4426950408889634

VMEM = pl.BlockSpec(memory_space=pltpu.VMEM)
SMEM = pl.BlockSpec(memory_space=pltpu.SMEM)
HBM = pl.BlockSpec(memory_space=pltpu.HBM)
ANY = pl.BlockSpec(memory_space=pl.ANY)
LIMIT = 24 * 1024 * 1024


def attend(query, kv_refs, source, token_dev, length, cache_rows, new_rows):
    key_rows = cache_rows + new_rows
    if len(kv_refs) == 1:
        keys, values = kv_refs[0][0:key_rows, :], kv_refs[0][key_rows : 2 * key_rows, :]
    else:
        old, fresh_rows = kv_refs
        keys = jnp.concatenate([old[0:cache_rows, :], fresh_rows[0:new_rows, :]], 0)
        values = jnp.concatenate([old[cache_rows:, :], fresh_rows[new_rows:, :]], 0)
    scores = lax.dot_general(
        keys, query, (((1,), (1,)), ((), ())), preferred_element_type=jnp.float32
    )
    rows = query.shape[0]
    slot = lax.broadcasted_iota(jnp.int32, (cache_rows, rows), 0)
    cached = jnp.where(slot < length - source * cache_rows, scores[:cache_rows], LOW)
    new = lax.broadcasted_iota(jnp.int32, (new_rows, rows), 0) + source * new_rows
    token = lax.rem(
        lax.broadcasted_iota(jnp.int32, (new_rows, rows), 1), new_rows
    ) + token_dev * new_rows
    fresh = jnp.where(new <= token, scores[cache_rows:], LOW)
    scores = jnp.concatenate([cached, fresh], 0)
    top = jnp.max(scores, axis=0, keepdims=True)
    weights = jnp.exp2((scores - top) * SLOPE)
    total = jnp.sum(weights, axis=0, keepdims=True)
    summed = lax.dot_general(
        values,
        weights.astype(jnp.bfloat16),
        (((0,), (0,)), ((), ())),
        preferred_element_type=jnp.float32,
    )
    return top, total, summed


def joined(one, two):
    top = jnp.maximum(one[0], two[0])
    left, right = jnp.exp2((one[0] - top) * SLOPE), jnp.exp2((two[0] - top) * SLOPE)
    return top, one[1] * left + two[1] * right, one[2] * left + two[2] * right


def stacked_heads(q_ref, first, count):
    return jnp.concatenate(
        [q_ref[:, pl.ds((first + g) * HEAD_DIM, HEAD_DIM)] for g in range(count)], 0
    )


def load_state(ref, lanes):
    return (
        ref[HEAD_DIM : HEAD_DIM + 1, lanes],
        ref[HEAD_DIM + 1 : HEAD_DIM + 2, lanes],
        ref[0:HEAD_DIM, lanes],
    )


def store_state(ref, lanes, state):
    top, total, summed = state
    ref[0:HEAD_DIM, lanes] = summed
    ref[HEAD_DIM : HEAD_DIM + 1, lanes] = top
    ref[HEAD_DIM + 1 : HEAD_DIM + 2, lanes] = total


def store_own(ref, lanes, state):
    top, total, summed = state
    ref[0:HEAD_DIM, lanes] = summed * (1.0 / total)
    ref[HEAD_DIM : HEAD_DIM + 1, lanes] = top * SLOPE + jnp.log2(total)


def store_sent(ref, blocks):
    row = lax.broadcasted_iota(jnp.int32, (ref.shape[0] - len(blocks) * HEAD_DIM, HEAD_DIM), 0)
    stats = jnp.zeros(row.shape, jnp.float32)
    for n, (top, total, summed) in enumerate(blocks):
        log = top * SLOPE + jnp.log2(total)
        high = log.astype(jnp.bfloat16).astype(jnp.float32)
        rest = log - high
        middle = rest.astype(jnp.bfloat16).astype(jnp.float32)
        for i, part in enumerate((high, middle, rest - middle)):
            stats = jnp.where(row == 3 * n + i, part, stats)
        ref[n * HEAD_DIM : (n + 1) * HEAD_DIM, :] = (summed * (1.0 / total)).astype(jnp.bfloat16)
    ref[len(blocks) * HEAD_DIM :, :] = stats.astype(jnp.bfloat16)


def sent_rows(blocks):
    return blocks * HEAD_DIM + -(-3 * blocks // 16) * 16


def attend_kernel(dims, blocks, q_xor, store, carried, len_ref, q_ref, *refs):
    cache_rows, new_rows, step = dims
    out_ref, kv_refs = refs[-1], []
    for _, count in blocks:
        kv_refs.append(refs[:count])
        refs = refs[count:]
    me = lax.axis_index("ctx")
    groups = q_ref.shape[1] // HEAD_DIM
    sent = []
    for at in range(0, groups, step):
        query = stacked_heads(q_ref, at, step)
        lanes = pl.ds(at * new_rows, step * new_rows)
        state = load_state(refs[0], lanes) if carried else None
        for (block, _), kv_ref in zip(blocks, kv_refs):
            ours = attend(
                query, kv_ref, me ^ block, me ^ q_xor, len_ref[0], cache_rows, new_rows
            )
            state = ours if state is None else joined(state, ours)
        if store == "state":
            store_state(out_ref, lanes, state)
        elif store == "own":
            store_own(out_ref, lanes, state)
        else:
            for lane in range(0, step * new_rows, HEAD_DIM):
                sent.append([part[:, lane : lane + HEAD_DIM] for part in state])
    if store == "sent":
        store_sent(out_ref, sent)


def merge_kernel(dims, columns, own_ref, got_ref, *refs):
    cache_rows, new_rows, _ = dims
    out_ref, block_ref, sem = refs[-3:]
    first, own_first, groups = columns
    pair = HEAD_DIM // new_rows
    stats = got_ref[groups // pair * HEAD_DIM :, :].astype(jnp.float32)
    for at in range(0, groups, pair):
        own_lanes = pl.ds((own_first + at) * new_rows, pair * new_rows)
        n = at // pair
        theirs = sum(stats[3 * n + i : 3 * n + i + 1] for i in range(3))
        mine = own_ref[HEAD_DIM : HEAD_DIM + 1, own_lanes]
        top = jnp.maximum(mine, theirs)
        left, right = jnp.exp2(mine - top), jnp.exp2(theirs - top)
        scale = 1.0 / (left + right)
        whole = own_ref[0:HEAD_DIM, own_lanes] * (left * scale) + got_ref[
            n * HEAD_DIM : (n + 1) * HEAD_DIM, :
        ].astype(jnp.float32) * (right * scale)
        turned = whole.T.astype(jnp.bfloat16)
        for g in range(pair):
            column = (at + g) * HEAD_DIM
            block_ref[:, column : column + HEAD_DIM] = turned[g * new_rows : (g + 1) * new_rows, :]
    copy = pltpu.make_async_copy(
        block_ref, out_ref.at[:, pl.ds(first * HEAD_DIM, groups * HEAD_DIM)], sem
    )
    copy.start()
    copy.wait()


def pack_kernel(head, apart, q_ref, ck_ref, cv_ref, nk_ref, nv_ref, *refs):
    sems, outs = refs[-1], refs[-3 - apart : -1]
    cache_rows, new_rows = ck_ref.shape[0], nk_ref.shape[0]
    key_rows = cache_rows + new_rows
    columns = pl.ds(head * HEAD_DIM, HEAD_DIM)
    if apart:
        places = ((0, 0), (0, cache_rows), (1, 0), (1, new_rows))
    else:
        places = ((0, 0), (0, key_rows), (0, cache_rows), (0, key_rows + cache_rows))
    copies = [
        (source.at[:, columns], outs[array].at[pl.ds(at, source.shape[0]), :])
        for source, (array, at) in zip((ck_ref, cv_ref, nk_ref, nv_ref), places)
    ]
    width = outs[-1].shape[1]
    copies.append((q_ref.at[:, pl.ds(head * width, width)], outs[-1]))
    handles = [
        pltpu.make_async_copy(source, target, sems.at[n])
        for n, (source, target) in enumerate(copies)
    ]
    for handle in handles:
        handle.start()
    for handle in handles:
        handle.wait()


def traded(value, xor, onward=False):
    pairs = [(source, source ^ xor) for source in range(lax.axis_size("ctx"))]
    return lax.ppermute(value, "ctx", [(a, b) for a, b in pairs if a < b or not onward])


def local_four(queries, cache_keys, cache_values, new_keys, new_values, prefix_len):
    cache_rows, kv_width = cache_keys.shape
    new_rows = queries.shape[0]
    heads = kv_width // HEAD_DIM
    groups = queries.shape[1] // kv_width
    key_rows = cache_rows + new_rows
    dims = (cache_rows, new_rows, groups)
    bf16, f32 = jnp.bfloat16, jnp.float32
    shape = jax.ShapeDtypeStruct
    arguments = [
        pltpu.with_memory_space_constraint(argument, pltpu.HBM)
        for argument in (queries, cache_keys, cache_values, new_keys, new_values)
    ]

    def pack(head, apart, after):
        rows = [2 * cache_rows, 2 * new_rows] if apart else [2 * key_rows]
        return pl.pallas_call(
            functools.partial(pack_kernel, head, apart),
            out_shape=[pltpu.VMEM((n, HEAD_DIM), bf16) for n in rows]
            + [pltpu.VMEM((new_rows, groups * HEAD_DIM), bf16)],
            in_specs=[HBM] * 5 + [ANY] * len(after),
            out_specs=[VMEM] * (len(rows) + 1),
            scratch_shapes=[pltpu.SemaphoreType.DMA((5,))],
            compiler_params=pltpu.CompilerParams(vmem_limit_bytes=2 * 1024 * 1024),
            name="pack",
        )(*arguments, *after)

    def work(query, blocks, q_xor, store, state=None, after=()):
        rows = query.shape[1] // HEAD_DIM * new_rows
        pairs = key_rows * rows * len(blocks)
        if store == "sent":
            out = pltpu.VMEM((sent_rows(rows // HEAD_DIM), HEAD_DIM), bf16)
        else:
            out = pltpu.VMEM((HEAD_DIM + 8, rows), f32)
        carried = () if state is None else (state,)
        refs = [r for _, ref in blocks for r in ref]
        return pl.pallas_call(
            functools.partial(
                attend_kernel, dims, tuple((b, len(ref)) for b, ref in blocks), q_xor, store, bool(carried)
            ),
            out_shape=out,
            in_specs=[SMEM] + [VMEM] * (1 + len(refs) + len(carried)) + [ANY] * len(after),
            out_specs=VMEM,
            compiler_params=pltpu.CompilerParams(vmem_limit_bytes=LIMIT),
            cost_estimate=pl.CostEstimate(
                flops=4 * HEAD_DIM * pairs * 40, bytes_accessed=1 << 20, transcendentals=pairs
            ),
            name="work",
        )(prefix_len, query, *refs, *carried, *after)

    def merge(own, got, columns, out=None, after=()):
        aliased = () if out is None else (out,)
        return pl.pallas_call(
            functools.partial(merge_kernel, dims, columns),
            out_shape=shape(queries.shape, bf16),
            in_specs=[VMEM] * 2 + [HBM] * len(aliased) + [ANY] * len(after),
            out_specs=HBM,
            scratch_shapes=[
                pltpu.VMEM((new_rows, columns[2] * HEAD_DIM), bf16),
                pltpu.SemaphoreType.DMA(()),
            ],
            compiler_params=pltpu.CompilerParams(vmem_limit_bytes=LIMIT),
            input_output_aliases={2: 0} if aliased else {},
            name="merge",
        )(own, got, *aliased, *after)

    kv0, q0 = pack(0, 0, ())
    far_kv0, far_q0 = traded(kv0, 1), traded(q0, 2)
    old1, new1, q1 = pack(1, 1, (kv0,))
    far_new1 = traded(new1, 2, True)
    far_old1 = traded(old1, 2)
    mine0 = work(q0, [(0, (kv0,))], 0, "state", after=(old1,))
    mine1 = work(q1, [(0, (old1, new1))], 0, "state", after=(mine0,))
    sent_q1, mine1 = lax.optimization_barrier((q1, mine1))
    far_q1 = traded(sent_q1, 1)
    theirs0 = work(far_q0, [(0, (kv0,))], 2, "state", after=(mine1,))
    sent0 = work(far_q0, [(1, (far_kv0,))], 2, "sent", state=theirs0, after=(mine1,))
    got0 = traded(sent0, 2)
    sent1 = work(far_q1, [(0, (old1, new1)), (2, (far_old1, far_new1))], 1, "sent", after=(sent0,))
    got1 = traded(sent1, 1)
    own0 = work(q0, [(1, (far_kv0,))], 0, "own", state=mine0, after=(sent1,))
    own1 = work(q1, [(2, (far_old1, far_new1))], 0, "own", state=mine1, after=(own0,))
    out = merge(own0, got0, (0, 0, groups), after=(own1,))
    return merge(own1, got1, (groups, 0, groups), out)


def passed_along(value, axis, steps):
    count = lax.axis_size(axis)
    pairs = [(source, (source + steps) % count) for source in range(count)]
    return lax.ppermute(value, axis, pairs)


def allowed_for(source, query_tok, cache_rows, query_rows, length):
    key_rows = cache_rows + query_rows
    key_index = jnp.arange(key_rows, dtype=jnp.int32)
    cache_pos = source * cache_rows + key_index
    new_pos = source * query_rows + key_index - cache_rows
    return jnp.where(
        (key_index < cache_rows)[None, :],
        (cache_pos < length)[None, :],
        new_pos[None, :] <= query_tok[:, None],
    )


def softmax_block(running, query_heads, kv_block, allowed):
    old_max, old_total, old_acc = running
    scale = HEAD_DIM ** (-0.5)
    scores = (
        jnp.einsum("hrd,hkd->hrk", query_heads, kv_block[0], preferred_element_type=jnp.float32)
        * scale
    )
    scores = jnp.where(allowed[None], scores, jnp.float32(-1e30))
    new_max = jnp.maximum(old_max, jnp.max(scores, -1))
    weights = jnp.where(allowed[None], jnp.exp(scores - new_max[..., None]), jnp.float32(0.0))
    rescale = jnp.exp(old_max - new_max)
    new_total = old_total * rescale + jnp.sum(weights, -1)
    new_acc = old_acc * rescale[..., None] + jnp.einsum(
        "hrk,hkd->hrd",
        weights.astype(jnp.bfloat16),
        kv_block[1],
        preferred_element_type=jnp.float32,
    )
    return (new_max, new_total, new_acc)


def empty_state(heads, rows):
    return (
        jnp.full((heads, rows), -1e30, jnp.float32),
        jnp.zeros((heads, rows), jnp.float32),
        jnp.zeros((heads, rows, HEAD_DIM), jnp.float32),
    )


def local_ring(queries, cache_keys, cache_values, new_keys, new_values, prefix_len):
    length = prefix_len[0]
    cycle_size = lax.axis_size("ctx")
    my_index = lax.axis_index("ctx")
    cache_rows = cache_keys.shape[0]
    query_rows = queries.shape[0]
    kv_width = cache_keys.shape[1]
    kv_heads = kv_width // HEAD_DIM
    groups = queries.shape[1] // kv_width
    key_rows = cache_rows + query_rows
    stacked = jnp.stack(
        [jnp.concatenate([cache_keys, new_keys], 0), jnp.concatenate([cache_values, new_values], 0)]
    )
    kv_block = stacked.reshape(2, key_rows, kv_heads, HEAD_DIM).transpose(0, 2, 1, 3)
    query_heads = (
        queries.reshape(query_rows, kv_heads, groups, HEAD_DIM)
        .transpose(1, 0, 2, 3)
        .reshape(kv_heads, query_rows * groups, HEAD_DIM)
    )
    query_tok = my_index * query_rows + jnp.arange(query_rows * groups, dtype=jnp.int32) // groups
    running = softmax_block(
        empty_state(kv_heads, query_rows * groups),
        query_heads,
        kv_block,
        allowed_for(my_index, query_tok, cache_rows, query_rows, length),
    )

    def one_turn(turn_index, loop_state):
        running_now, held = loop_state
        held = passed_along(held, "ctx", 1)
        source = (my_index - turn_index) % cycle_size
        allowed = allowed_for(source, query_tok, cache_rows, query_rows, length)
        return (softmax_block(running_now, query_heads, held, allowed), held)

    running, held = lax.fori_loop(1, cycle_size, one_turn, (running, kv_block))
    final_max, final_total, final_acc = running
    result = final_acc / final_total[..., None]
    result = result.reshape(kv_heads, query_rows, groups, HEAD_DIM).transpose(1, 0, 2, 3)
    return result.reshape(query_rows, kv_width * groups).astype(jnp.bfloat16)


def local(*arguments):
    if lax.axis_size("ctx") == 4 and arguments[1].shape[1] == 2 * HEAD_DIM:
        return local_four(*arguments)
    return local_ring(*arguments)


def solution(mesh):
    in_specs = (
        P(("dp", "ctx"), "tp"),
        P(("dp", "ctx"), "tp"),
        P(("dp", "ctx"), "tp"),
        P(("dp", "ctx"), "tp"),
        P(("dp", "ctx"), "tp"),
        P("dp"),
    )
    out_specs = P(("dp", "ctx"), "tp")
    return jax.shard_map(local, mesh=mesh, in_specs=in_specs, out_specs=out_specs, check_vma=False)
```
